32 devices in a mesh: row: 8 (over z, x), col: 2 (over y), depth: 2 (over core).
Axes of the slice: x: 2, y: 2, z: 4, core: 2. Of those that a mesh axis runs over, the one named last changes fastest.
Arguments:
- tokens: bfloat16 [64, 8192], P('row', ('col', 'depth')), may hold values from -6 to 6
- grad_out: bfloat16 [64, 8192], P('row', ('col', 'depth')), may hold values from -6 to 6
- gate_weight: bfloat16 [8192, 28672], P(('col', 'depth'), 'row'), may hold values from -0.0625 to 0.0625
- up_weight: bfloat16 [8192, 28672], P(('col', 'depth'), 'row'), may hold values from -0.0625 to 0.0625
- down_weight: bfloat16 [28672, 8192], P('row', ('col', 'depth')), may hold values from -0.03125 to 0.03125
Outputs:
- layer_out: bfloat16 [64, 8192], P('row', ('col', 'depth'))
- grad_tokens: bfloat16 [64, 8192], P('row', ('col', 'depth'))
- grad_gate: bfloat16 [8192, 28672], P(('col', 'depth'), 'row')
- grad_up: bfloat16 [8192, 28672], P(('col', 'depth'), 'row')
- grad_down: bfloat16 [28672, 8192], P('row', ('col', 'depth'))
The draws below stay inside these ranges and needn't reach their ends.
All inputs are finite; a program needn't handle non-finite values.
Results may differ from the reference program's by a relative error of at most 0.0049.
Values may be sent and summed in bfloat16 or wider, within the bound.
No kernel may reach another device: no remote copies, remote signals or barrier semaphores. Data moves between devices by JAX's collectives and lax.ppermute only.
A program may use at most 256 MiB of HBM per device.

```python
import jax
import jax.numpy as jnp

D = 8192
FF = 28672
TOKENS = 64


def block_levels(key, extent, cuts, smallest, largest):
    loudness, own = 1.0, jax.random.fold_in(key, 6)
    for axis_at, parts in cuts:
        draws = jnp.exp(jax.random.uniform(jax.random.fold_in(own, axis_at), (parts,), jnp.float32, smallest / len(cuts), largest / len(cuts)))
        loudness = loudness * jnp.repeat(draws, extent[axis_at] // parts).reshape([-1 if axis == axis_at else 1 for axis in range(len(extent))])
    return loudness


def centred(own_key, dims, spread, bound, shards=(), kind=jnp.bfloat16):
    gain = block_levels(own_key, dims, shards, -0.22, 0.18) if shards else 1.0
    result = jax.random.normal(own_key, dims, jnp.float32) * spread * gain
    return jnp.minimum(jnp.maximum(result, -bound), bound).astype(kind)


def setup_inputs(seed: int = 0) -> dict:
    key_list = jax.random.split(jax.random.key(seed), 6)
    return {
        "tokens": centred(key_list[0], (TOKENS, D), 1.0, 6.0, ((0, 8), (1, 4))),
        "grad_out": centred(key_list[1], (TOKENS, D), 1.0, 6.0, ((0, 8), (1, 4))),
        "gate_weight": centred(key_list[2], (D, FF), D ** -0.5, 0.0625, ((0, 4), (1, 8))),
        "up_weight": centred(key_list[3], (D, FF), D ** -0.5, 0.0625, ((0, 4), (1, 8))),
        "down_weight": centred(key_list[4], (FF, D), FF ** -0.5, 0.03125, ((0, 8), (1, 4))),
    }


def reference(tokens, grad_out, gate_weight, up_weight, down_weight):
    gate_pre = jnp.dot(tokens, gate_weight, preferred_element_type=jnp.float32)
    up_proj = jnp.dot(tokens, up_weight, preferred_element_type=jnp.float32)
    sigmoid_gate = jax.nn.sigmoid(gate_pre)
    activated = gate_pre * sigmoid_gate
    hidden = (activated * up_proj).astype(jnp.bfloat16)
    layer_out = jnp.dot(hidden, down_weight, preferred_element_type=jnp.float32).astype(jnp.bfloat16)
    d_hidden = jnp.dot(grad_out, down_weight.T, preferred_element_type=jnp.float32)
    d_gate = (d_hidden * up_proj * sigmoid_gate * (1.0 + gate_pre * (1.0 - sigmoid_gate))).astype(jnp.bfloat16)
    d_up = (d_hidden * activated).astype(jnp.bfloat16)
    grad_down = jnp.dot(hidden.T, grad_out, preferred_element_type=jnp.float32).astype(jnp.bfloat16)
    grad_gate = jnp.dot(tokens.T, d_gate, preferred_element_type=jnp.float32).astype(jnp.bfloat16)
    grad_up = jnp.dot(tokens.T, d_up, preferred_element_type=jnp.float32).astype(jnp.bfloat16)
    grad_tokens = (jnp.dot(d_gate, gate_weight.T, preferred_element_type=jnp.float32)
                   + jnp.dot(d_up, up_weight.T, preferred_element_type=jnp.float32)).astype(jnp.bfloat16)
    return layer_out, grad_tokens, grad_gate, grad_up, grad_down
```

```python
import functools

import jax
import jax.numpy as jnp
from jax import lax
from jax.experimental import pallas as pl
from jax.experimental.pallas import tpu as pltpu
from jax.sharding import PartitionSpec as P

BF16 = jnp.bfloat16
F32 = jnp.float32
IN_VMEM = pl.BlockSpec(memory_space=pltpu.VMEM)
IN_SMEM = pl.BlockSpec(memory_space=pltpu.SMEM)
ANYWHERE = pl.BlockSpec(memory_space=pl.ANY)
MIB = 1 << 20


def params(mib):
    return pltpu.CompilerParams(vmem_limit_bytes=mib * MIB)


def cost(flops=0, moved=0, exps=0):
    return pl.CostEstimate(flops=flops, bytes_accessed=moved, transcendentals=exps)


def in_vmem(array):
    return pltpu.with_memory_space_constraint(array, pltpu.VMEM)


def in_hbm(array):
    return pltpu.with_memory_space_constraint(array, pltpu.HBM)


def swap(array, axis, distance):
    size = lax.axis_size(axis)
    return lax.ppermute(array, axis, [(i, i ^ distance) for i in range(size)])


def tile_of(extent, largest):
    best = 128
    for tile in range(128, largest + 1, 128):
        if extent % tile == 0:
            best = tile
    return best


def contract_cols(left, right):
    return lax.dot_general(left, right, (((1,), (1,)), ((), ())), preferred_element_type=F32)


def contract_rows(left, right):
    return lax.dot_general(left, right, (((0,), (0,)), ((), ())), preferred_element_type=F32)


def through(arrays, first_input, first_output):
    shapes = [pltpu.VMEM(a.shape, a.dtype) for a in arrays]
    return shapes, {first_input + i: first_output + i for i in range(len(arrays))}


def load(weight, held, after=()):
    parts = 4
    step = weight.shape[0] // parts

    def kernel(src, *refs):
        dst, sem = refs[len(held) + len(after)], refs[-1]
        copies = []
        for i in range(parts):
            rows = pl.ds(i * step, step)
            copies.append(pltpu.make_async_copy(src.at[rows], dst.at[rows], sem.at[i]))
            copies[-1].start()
        for copy in copies:
            copy.wait()

    shapes, aliases = through(held, 1, 1)
    return pl.pallas_call(
        kernel,
        out_shape=[pltpu.VMEM(weight.shape, weight.dtype)] + shapes,
        in_specs=[ANYWHERE] + [IN_VMEM] * len(held) + [ANYWHERE] * len(after),
        out_specs=[IN_VMEM] * (1 + len(held)),
        scratch_shapes=[pltpu.SemaphoreType.DMA((parts,))],
        input_output_aliases=aliases,
        compiler_params=params(3),
        cost_estimate=cost(moved=weight.size * 2),
        name="load_weight",
    )(in_hbm(weight), *[in_vmem(a) for a in held], *after)


def join(own, near):
    own_rows, features = own[0].shape

    def kernel(*refs):
        for g in range(2):
            both = [refs[g][...].astype(F32), refs[2 + g][...].astype(F32)]
            rows = slice(2 * g * own_rows, 2 * (g + 1) * own_rows)
            refs[4][rows, :] = jnp.concatenate(both, axis=0).astype(BF16)

    return pl.pallas_call(
        kernel,
        out_shape=pltpu.VMEM((4 * own_rows, features), BF16),
        in_specs=[IN_VMEM] * 4,
        out_specs=IN_VMEM,
        compiler_params=params(3),
        name="join",
    )(*own, *near)


def unpack(blocks, held):
    n, w = len(blocks), len(held)
    rows, features = blocks[0].shape
    half = rows // 2

    def kernel(*refs):
        for b in range(n):
            for g in range(2):
                refs[n + w + g][b * half : (b + 1) * half, :] = refs[b][g * half : (g + 1) * half, :]

    shapes, aliases = through(held, n, 2)
    results = pl.pallas_call(
        kernel,
        out_shape=[pltpu.VMEM((n * half, features), BF16)] * 2 + shapes,
        in_specs=[IN_VMEM] * (n + w),
        out_specs=[IN_VMEM] * (2 + w),
        input_output_aliases=aliases,
        compiler_params=params(3),
        name="unpack",
    )(*blocks, *[in_vmem(a) for a in held])
    return results[0], results[1], results[2:]


def first_products(place, x, weights, used, offset, width, groups, transposed):
    total = x.shape[0]
    share = total // groups
    n, w = len(used), len(weights)

    def kernel(place_ref, x_ref, *refs):
        outs, acc = refs[w : w + groups], refs[-1]
        for g in range(n):
            weight = refs[used[g]]
            if transposed:
                acc[...] = contract_cols(x_ref[...], weight[offset : offset + width, :])
            else:
                acc[...] = jnp.dot(
                    x_ref[...], weight[:, offset : offset + width], preferred_element_type=F32
                )
            for j in range(groups):
                at = pl.multiple_of((place_ref[0] ^ j) * share, share)
                outs[j][g] = acc[pl.ds(at, share), :]

    results = pl.pallas_call(
        kernel,
        out_shape=[pltpu.VMEM((n, share, width), F32)] * groups
        + [pltpu.VMEM(a.shape, a.dtype) for a in weights],
        in_specs=[IN_SMEM] + [IN_VMEM] * (1 + w),
        out_specs=[IN_VMEM] * (groups + w),
        scratch_shapes=[pltpu.VMEM((total, width), F32)],
        input_output_aliases={2 + i: groups + i for i in range(w)},
        compiler_params=params(3),
        name="first_products",
    )(place, x, *[in_vmem(a) for a in weights])
    return results[:groups], results[groups:]


def core_sum(parts, weights):
    n, w = len(parts), len(weights)

    def kernel(*refs):
        total = refs[0][...]
        for ref in refs[1:n]:
            total = total + ref[...]
        refs[n + w][...] = total
        refs[n + w + 1][...] = total.astype(BF16)

    shape = parts[0].shape
    results = pl.pallas_call(
        kernel,
        out_shape=[pltpu.VMEM(shape, F32), pltpu.VMEM(shape, BF16)]
        + [pltpu.VMEM(a.shape, a.dtype) for a in weights],
        in_specs=[IN_VMEM] * (n + w),
        out_specs=[IN_VMEM] * (2 + w),
        input_output_aliases={n + i: 2 + i for i in range(w)},
        compiler_params=params(3),
        name="core_sum",
    )(*parts, *[in_vmem(a) for a in weights])
    return results[:2], results[2:]


def activations(gate_up, back, offset, width, weights):
    n, w = len(gate_up), len(weights)
    share = gate_up[0].shape[1]

    def kernel(*refs):
        gu, bk, out = refs[:n], refs[n : 2 * n], refs[2 * n + w]

        def added(group, g, cols):
            total = group[0][g, :, cols]
            for ref in group[1:]:
                total = total + ref[g, :, cols].astype(F32)
            return total

        gate_pre = added(gu, 0, slice(None))
        up_proj = added(gu, 1, slice(None))
        d_hidden = added(bk, 0, slice(offset, offset + width))
        sigmoid_gate = 1.0 / (1.0 + jnp.exp(-gate_pre))
        activated = gate_pre * sigmoid_gate
        out[0] = (activated * up_proj).astype(BF16)
        out[1] = (
            d_hidden * up_proj * sigmoid_gate * (1.0 + gate_pre * (1.0 - sigmoid_gate))
        ).astype(BF16)
        out[2] = (d_hidden * activated).astype(BF16)

    results = pl.pallas_call(
        kernel,
        out_shape=[pltpu.VMEM((3, share, width), BF16)]
        + [pltpu.VMEM(a.shape, a.dtype) for a in weights],
        in_specs=[IN_VMEM] * (2 * n + w),
        out_specs=[IN_VMEM] * (1 + w),
        input_output_aliases={2 * n + i: 1 + i for i in range(w)},
        compiler_params=params(3),
        name="activations",
    )(*gate_up, *back, *[in_vmem(a) for a in weights])
    return results[0], results[1:]


def second_products(place, shares, weights, offset, width, before, last, own_rows):
    groups = len(shares)
    share = shares[0].shape[1]
    total = share * groups
    features = weights[0].shape[0]
    blocks = total // own_rows

    def kernel(place_ref, *refs):
        share_refs = refs[:groups]
        gate_ref, up_ref, down_ref = refs[groups : groups + 3]
        before_refs = refs[groups + 3 : groups + 3 + len(before)]
        rest = refs[groups + 3 + len(before) :]
        laid = rest[0]
        for j in range(groups):
            at = pl.multiple_of((place_ref[0] ^ j) * share, share)
            laid[:, pl.ds(at, share), :] = share_refs[j][...]
        cols = slice(offset, offset + width)
        out = jnp.dot(laid[0], down_ref[cols, :], preferred_element_type=F32)
        back = contract_cols(laid[1], gate_ref[:, cols]) + contract_cols(laid[2], up_ref[:, cols])
        if before:
            out = out + before_refs[0][0]
            back = back + before_refs[0][1]
        if not last:
            rest[1][0] = out
            rest[1][1] = back
        else:
            keep, send = rest[1:3]
            for b in range(blocks):
                rows = slice(b * own_rows, (b + 1) * own_rows)
                both = jnp.concatenate([out[rows], back[rows]], axis=0)
                if b % 2:
                    send[b // 2] = both.astype(BF16)
                else:
                    keep[b // 2] = both

    if last:
        sums = [
            pltpu.VMEM((blocks // 2, 2 * own_rows, features), F32),
            pltpu.VMEM((blocks // 2, 2 * own_rows, features), BF16),
        ]
    else:
        sums = [pltpu.VMEM((2, total, features), F32)]
    kept = [] if last else [pltpu.VMEM(w.shape, w.dtype) for w in weights]
    results = pl.pallas_call(
        kernel,
        out_shape=[pltpu.VMEM((3, total, width), BF16)] + sums + kept,
        in_specs=[IN_SMEM] + [IN_VMEM] * (groups + 3 + len(before)),
        out_specs=[IN_VMEM] * (1 + len(sums) + len(kept)),
        input_output_aliases={1 + groups + g: 1 + len(sums) + g for g in range(len(kept))},
        compiler_params=params(3),
        name="second_products",
    )(place, *shares, *[in_vmem(w) for w in weights], *before)
    return results[0], results[1 : 1 + len(sums)], results[1 + len(sums) :]


def row_sum(keep, near, after):
    n = keep.shape[0]

    def kernel(keep_ref, near_ref, *refs):
        refs = refs[len(after) :]
        refs[0][...] = keep_ref[0] + near_ref[0].astype(F32)
        for j in range(1, n):
            refs[j][...] = (keep_ref[j] + near_ref[j].astype(F32)).astype(BF16)

    shape = keep.shape[1:]
    results = pl.pallas_call(
        kernel,
        out_shape=[pltpu.VMEM(shape, F32)] + [pltpu.VMEM(shape, BF16)] * (n - 1),
        in_specs=[IN_VMEM] * 2 + [ANYWHERE] * len(after),
        out_specs=[IN_VMEM] * n,
        compiler_params=params(3),
        name="row_sum",
    )(keep, near, *[in_hbm(a) for a in after])
    return results[0], results[1:]


def last_sum(total, far, after):
    n = len(far)
    both, features = total.shape

    def kernel(total_ref, *refs):
        outs = refs[n + len(after) :]
        value = total_ref[...]
        for ref in refs[:n]:
            value = value + ref[...].astype(F32)
        outs[0][...] = value[: both // 2].astype(BF16)
        outs[1][...] = value[both // 2 :].astype(BF16)

    return pl.pallas_call(
        kernel,
        out_shape=[jax.ShapeDtypeStruct((both // 2, features), BF16)] * 2,
        in_specs=[IN_VMEM] * (1 + n) + [ANYWHERE] * len(after),
        out_specs=[IN_VMEM] * 2,
        compiler_params=params(3),
        name="last_sum",
    )(total, *far, *[in_hbm(a) for a in after])


def outer_rows(x, laid, which, offsets, after=()):
    features = x.shape[1]
    widths = [a.shape[2] for a in laid]
    hidden = sum(widths)
    tile = tile_of(features, 256)
    slots = min(4, features // tile)
    n = len(laid)

    def kernel(x_ref, *refs):
        laid_refs = refs[:n]
        out, stage, sems = refs[n + len(after) :]

        def sent(slot, at):
            return pltpu.make_async_copy(stage.at[slot], out.at[pl.ds(at, tile)], sems.at[slot])

        @pl.loop(0, features // tile)
        def _(i):
            slot = lax.rem(i, slots)

            @pl.when(i >= slots)
            def _():
                sent(slot, 0).wait()

            at = pl.multiple_of(i * tile, tile)
            left = x_ref[:, pl.ds(at, tile)]
            for c in range(n):
                step = tile_of(widths[c], 512)
                for s in range(0, widths[c], step):
                    stage[slot, :, offsets[c] + s : offsets[c] + s + step] = contract_rows(
                        left, laid_refs[c][which, :, s : s + step]
                    ).astype(BF16)
            sent(slot, at).start()

        for slot in range(slots):
            sent(slot, 0).wait()

    return pl.pallas_call(
        kernel,
        out_shape=jax.ShapeDtypeStruct((features, hidden), BF16),
        in_specs=[IN_VMEM] * (1 + n) + [ANYWHERE] * len(after),
        out_specs=ANYWHERE,
        scratch_shapes=[
            pltpu.VMEM((slots, tile, hidden), BF16),
            pltpu.SemaphoreType.DMA((slots,)),
        ],
        compiler_params=params(12),
        cost_estimate=cost(moved=features * hidden * 2),
        name="outer_rows",
    )(x, *laid, *after)


def outer_down(grad, laid, offsets, after=()):
    features = grad.shape[1]
    widths = [a.shape[2] for a in laid]
    hidden = sum(widths)
    tiles = [tile_of(w, 256) for w in widths]
    tile = min(tiles)
    n = len(laid)
    slots = min(4, min(w // tile for w in widths))
    step = tile_of(features, 512)

    def kernel(grad_ref, *refs):
        laid_refs = refs[:n]
        out, stage, sems = refs[n + len(after) :]

        def sent(slot, at):
            return pltpu.make_async_copy(stage.at[slot], out.at[pl.ds(at, tile)], sems.at[slot])

        for c in range(n):

            @pl.loop(0, widths[c] // tile)
            def _(i):
                slot = lax.rem(i + offsets[c] // tile, slots)

                if c:
                    sent(slot, 0).wait()
                else:

                    @pl.when(i >= slots)
                    def _():
                        sent(slot, 0).wait()

                at = pl.multiple_of(i * tile, tile)
                left = laid_refs[c][0, :, pl.ds(at, tile)]
                for s in range(0, features, step):
                    stage[slot, :, s : s + step] = contract_rows(
                        left, grad_ref[:, s : s + step]
                    ).astype(BF16)
                sent(slot, offsets[c] + at).start()

        for slot in range(slots):
            sent(slot, 0).wait()

    return pl.pallas_call(
        kernel,
        out_shape=jax.ShapeDtypeStruct((hidden, features), BF16),
        in_specs=[IN_VMEM] * (1 + n) + [ANYWHERE] * len(after),
        out_specs=ANYWHERE,
        scratch_shapes=[
            pltpu.VMEM((slots, tile, features), BF16),
            pltpu.SemaphoreType.DMA((slots,)),
        ],
        compiler_params=params(12),
        cost_estimate=cost(moved=features * hidden * 2),
        name="outer_down",
    )(grad, *laid, *after)


def per_device(tokens, grad_out, gate_weight, up_weight, down_weight):
    own_rows = tokens.shape[0]
    rows, cores, chips = (lax.axis_size(a) for a in ("row", "depth", "col"))
    hidden = gate_weight.shape[1]
    place = lax.axis_index("depth").astype(jnp.int32).reshape(1)

    own = [tokens, grad_out]
    near = [swap(a, "row", 1) for a in own]
    (down,) = load(down_weight, [])
    pair = join(own, near)
    blocks = [pair] + [swap(pair, "row", k) for k in range(2, rows, 2)]
    gate, down = load(gate_weight, [down], (pair,))
    up, gate, down = load(up_weight, [gate, down])
    tok_all, grad_all, weights = unpack(blocks, [gate, up, down])

    def over_cores(parts):
        return [parts[0]] + [swap(parts[j], "depth", j) for j in range(1, cores)]

    def over_chips(total, rounded):
        return [total] + [swap(rounded, "col", k) for k in range(1, chips)]

    tiles = hidden // 128
    cut = 128 * (tiles // 2)
    spans = [(0, cut), (cut, hidden - cut)]
    offsets = [s[0] for s in spans]

    part_back, weights = first_products(place, grad_all, weights, [2], 0, hidden, cores, True)
    part_back = over_cores(part_back)
    parts = []
    for c, (offset, width) in enumerate(spans):
        part, weights = first_products(
            place, tok_all, weights, [0, 1], offset, width, cores, False
        )
        parts.append(over_cores(part))
        if not c:
            sums, weights = core_sum(part_back, weights)
            back = over_chips(*sums)
    gate_up = []
    for part in parts:
        sums, weights = core_sum(part, weights)
        gate_up.append(over_chips(*sums))

    laid, before = [], []
    for c, (offset, width) in enumerate(spans):
        acts, weights = activations(gate_up[c], back, offset, width, weights)
        shares = [acts] + [swap(acts, "depth", j) for j in range(1, cores)]
        here, before, weights = second_products(
            place, shares, weights, offset, width, before, c == len(spans) - 1, own_rows
        )
        laid.append(here)

    keep, send = before
    near = swap(send, "row", 1)
    grad_down = outer_down(grad_all, laid, offsets, (send,))
    total, rounded = row_sum(keep, near, (grad_down,))
    far = [swap(rounded[j - 1], "row", 2 * j) for j in range(1, rows // 2)]
    grad_gate = outer_rows(tok_all, laid, 1, offsets, (total,))
    grad_up = outer_rows(tok_all, laid, 2, offsets, (in_hbm(grad_gate),))
    layer_out, grad_tokens = last_sum(total, far, (grad_up,))
    return layer_out, grad_tokens, grad_gate, grad_up, grad_down


def solution(mesh):
    acts = P("row", ("col", "depth"))
    wide = P(("col", "depth"), "row")
    return jax.shard_map(
        per_device,
        mesh=mesh,
        in_specs=(acts, acts, wide, wide, acts),
        out_specs=(acts, acts, wide, wide, acts),
        check_vma=False,
    )
```

```python
import functools

import jax
import jax.numpy as jnp
from jax import lax
from jax.experimental import pallas as pl
from jax.experimental.pallas import tpu as pltpu
from jax.sharding import PartitionSpec as P

BF16 = jnp.bfloat16
F32 = jnp.float32
IN_VMEM = pl.BlockSpec(memory_space=pltpu.VMEM)
IN_SMEM = pl.BlockSpec(memory_space=pltpu.SMEM)
ANYWHERE = pl.BlockSpec(memory_space=pl.ANY)
MIB = 1 << 20


def params(mib):
    return pltpu.CompilerParams(vmem_limit_bytes=mib * MIB)


def cost(flops=0, moved=0, exps=0):
    return pl.CostEstimate(flops=flops, bytes_accessed=moved, transcendentals=exps)


def in_vmem(array):
    return pltpu.with_memory_space_constraint(array, pltpu.VMEM)


def in_hbm(array):
    return pltpu.with_memory_space_constraint(array, pltpu.HBM)


def swap(array, axis, distance):
    size = lax.axis_size(axis)
    return lax.ppermute(array, axis, [(i, i ^ distance) for i in range(size)])


def tile_of(extent, largest):
    best = 128
    for tile in range(128, largest + 1, 128):
        if extent % tile == 0:
            best = tile
    return best


def contract_cols(left, right):
    return lax.dot_general(left, right, (((1,), (1,)), ((), ())), preferred_element_type=F32)


def contract_rows(left, right):
    return lax.dot_general(left, right, (((0,), (0,)), ((), ())), preferred_element_type=F32)


def through(arrays, first_input, first_output):
    shapes = [pltpu.VMEM(a.shape, a.dtype) for a in arrays]
    return shapes, {first_input + i: first_output + i for i in range(len(arrays))}


def make_room(weight, held):
    shapes, aliases = through(held, 0, 1)
    results = pl.pallas_call(
        lambda *refs: None,
        out_shape=[pltpu.VMEM(weight.shape, weight.dtype)] + shapes,
        in_specs=[IN_VMEM] * len(held),
        out_specs=[IN_VMEM] * (1 + len(held)),
        input_output_aliases=aliases,
        compiler_params=params(4),
        name="make_room",
    )(*[in_vmem(a) for a in held])
    return results[0], results[1:]


def load(weight, held, after=()):
    parts = 4
    step = weight.shape[0] // parts

    def kernel(src, *refs):
        dst, sem = refs[len(held) + len(after)], refs[-1]
        copies = []
        for i in range(parts):
            rows = pl.ds(i * step, step)
            copies.append(pltpu.make_async_copy(src.at[rows], dst.at[rows], sem.at[i]))
            copies[-1].start()
        for copy in copies:
            copy.wait()

    shapes, aliases = through(held, 1, 1)
    results = pl.pallas_call(
        kernel,
        out_shape=[pltpu.VMEM(weight.shape, weight.dtype)] + shapes,
        in_specs=[ANYWHERE] + [IN_VMEM] * len(held) + [ANYWHERE] * len(after),
        out_specs=[IN_VMEM] * (1 + len(held)),
        scratch_shapes=[pltpu.SemaphoreType.DMA((parts,))],
        input_output_aliases=aliases,
        compiler_params=params(4),
        cost_estimate=cost(moved=weight.size * 2),
        name="load_weight",
    )(in_hbm(weight), *[in_vmem(a) for a in held], *after)
    return results[0], results[1:]


def pack(tokens, grad_out):
    own_rows, features = tokens.shape

    def kernel(tok_ref, grad_ref, out, stage, sems):
        copies = [
            pltpu.make_async_copy(ref, stage.at[i], sems.at[i])
            for i, ref in enumerate((tok_ref, grad_ref))
        ]
        for copy in copies:
            copy.start()
        for copy in copies:
            copy.wait()
        both = [stage[0].astype(F32), stage[1].astype(F32)]
        out[...] = jnp.concatenate(both, axis=0).astype(BF16)

    return pl.pallas_call(
        kernel,
        out_shape=pltpu.VMEM((2 * own_rows, features), BF16),
        in_specs=[ANYWHERE] * 2,
        out_specs=IN_VMEM,
        scratch_shapes=[
            pltpu.VMEM((2, own_rows, features), BF16),
            pltpu.SemaphoreType.DMA((2,)),
        ],
        compiler_params=params(4),
        name="pack",
    )(in_hbm(tokens), in_hbm(grad_out))


def join(own, near):
    both, features = own.shape
    own_rows = both // 2

    def kernel(own_ref, near_ref, out):
        pair = [own_ref[...].astype(F32), near_ref[...].astype(F32)]
        for g in range(2):
            half = slice(g * own_rows, (g + 1) * own_rows)
            out[g * both : (g + 1) * both, :] = jnp.concatenate(
                [p[half] for p in pair], axis=0
            ).astype(BF16)

    return pl.pallas_call(
        kernel,
        out_shape=pltpu.VMEM((2 * both, features), BF16),
        in_specs=[IN_VMEM] * 2,
        out_specs=IN_VMEM,
        compiler_params=params(4),
        name="join",
    )(own, near)


def unpack(blocks, held):
    n, w = len(blocks), len(held)
    rows, features = blocks[0].shape
    half = rows // 2

    def kernel(*refs):
        for b in range(n):
            for g in range(2):
                refs[n + w + g][b * half : (b + 1) * half, :] = refs[b][g * half : (g + 1) * half, :]

    shapes, aliases = through(held, n, 2)
    results = pl.pallas_call(
        kernel,
        out_shape=[pltpu.VMEM((n * half, features), BF16)] * 2 + shapes,
        in_specs=[IN_VMEM] * (n + w),
        out_specs=[IN_VMEM] * (2 + w),
        input_output_aliases=aliases,
        compiler_params=params(4),
        name="unpack",
    )(*blocks, *[in_vmem(a) for a in held])
    return results[0], results[1], results[2:]


def back_products(place, x, source, weights, groups):
    total = x.shape[0]
    share = total // groups
    hidden = source.shape[0]
    tile = tile_of(hidden, 1024)
    n, w = hidden // tile, len(weights)

    def kernel(place_ref, x_ref, src, *refs):
        outs, dst, acc, sems = refs[w : w + groups], refs[2 * w + groups - 1], refs[-2], refs[-1]
        spans = [slice(b * tile, (b + 1) * tile) for b in range(n)]
        copies = [
            pltpu.make_async_copy(src.at[spans[b]], dst.at[spans[b]], sems.at[b]) for b in range(n)
        ]
        for copy in copies:
            copy.start()
        for b in range(n):
            copies[b].wait()
            acc[...] = contract_cols(x_ref[...], dst[spans[b], :])
            for j in range(groups):
                at = pl.multiple_of((place_ref[0] ^ j) * share, share)
                outs[j][:, spans[b]] = acc[pl.ds(at, share), :]

    shapes, aliases = through(weights, 3, groups)
    results = pl.pallas_call(
        kernel,
        out_shape=[pltpu.VMEM((share, hidden), F32)] * groups + shapes,
        in_specs=[IN_SMEM, IN_VMEM, ANYWHERE] + [IN_VMEM] * w,
        out_specs=[IN_VMEM] * (groups + w),
        scratch_shapes=[pltpu.VMEM((total, tile), F32), pltpu.SemaphoreType.DMA((n,))],
        input_output_aliases=aliases,
        compiler_params=params(4),
        name="back_products",
    )(place, x, in_hbm(source), *[in_vmem(a) for a in weights])
    return results[:groups], results[groups:]


def first_products(place, x, weights, used, offset, width, groups):
    total = x.shape[0]
    share = total // groups
    n, w = len(used), len(weights)

    def kernel(place_ref, x_ref, *refs):
        outs, acc = refs[w : w + groups], refs[-1]
        for g in range(n):
            acc[...] = jnp.dot(
                x_ref[...],
                refs[used[g]][:, offset : offset + width],
                preferred_element_type=F32,
            )
            for j in range(groups):
                at = pl.multiple_of((place_ref[0] ^ j) * share, share)
                outs[j][:, g * width : (g + 1) * width] = acc[pl.ds(at, share), :]

    shapes, aliases = through(weights, 2, groups)
    results = pl.pallas_call(
        kernel,
        out_shape=[pltpu.VMEM((share, n * width), F32)] * groups + shapes,
        in_specs=[IN_SMEM] + [IN_VMEM] * (1 + w),
        out_specs=[IN_VMEM] * (groups + w),
        scratch_shapes=[pltpu.VMEM((total, width), F32)],
        input_output_aliases=aliases,
        compiler_params=params(4),
        name="first_products",
    )(place, x, *[in_vmem(a) for a in weights])
    return results[:groups], results[groups:]


def core_sum(pieces, weights):
    widths = [parts[0].shape[1] for parts in pieces]
    share, columns = pieces[0][0].shape[0], sum(widths)
    flat = [part for parts in pieces for part in parts]
    n, w, groups = len(flat), len(weights), len(pieces[0])

    def kernel(*refs):
        at = 0
        for p, width in enumerate(widths):
            total = refs[p * groups][...]
            for ref in refs[p * groups + 1 : (p + 1) * groups]:
                total = total + ref[...]
            refs[n + w][:, at : at + width] = total
            refs[n + w + 1][:, at : at + width] = total.astype(BF16)
            at += width

    shapes, aliases = through(weights, n, 2)
    results = pl.pallas_call(
        kernel,
        out_shape=[pltpu.VMEM((share, columns), F32), pltpu.VMEM((share, columns), BF16)] + shapes,
        in_specs=[IN_VMEM] * (n + w),
        out_specs=[IN_VMEM] * (2 + w),
        input_output_aliases=aliases,
        compiler_params=params(4),
        name="core_sum",
    )(*flat, *[in_vmem(a) for a in weights])
    return results[:2], results[2:]


def added(refs, cols):
    total = refs[0][:, cols]
    for ref in refs[1:]:
        total = total + ref[:, cols].astype(F32)
    return total


def hidden_units(terms, held):
    n, w = len(terms), len(held)
    share, columns = terms[0].shape
    hidden = columns // 2
    step = tile_of(hidden, 512)

    def kernel(*refs):
        for at in range(0, hidden, step):
            gate_pre = added(refs[:n], slice(at, at + step))
            up_proj = added(refs[:n], slice(hidden + at, hidden + at + step))
            sigmoid_gate = 1.0 / (1.0 + jnp.exp(-gate_pre))
            refs[n + w][:, at : at + step] = (gate_pre * sigmoid_gate * up_proj).astype(BF16)

    shapes, aliases = through(held, n, 1)
    results = pl.pallas_call(
        kernel,
        out_shape=[pltpu.VMEM((share, hidden), BF16)] + shapes,
        in_specs=[IN_VMEM] * (n + w),
        out_specs=[IN_VMEM] * (1 + w),
        input_output_aliases=aliases,
        compiler_params=params(4),
        name="hidden_units",
    )(*terms, *[in_vmem(a) for a in held])
    return results[0], results[1:]


def gate_grads(terms, back_terms, held):
    n, w = len(terms), len(held)
    share, columns = terms[0].shape
    hidden = columns // 2
    step = tile_of(hidden, 512)

    def kernel(*refs):
        out = refs[2 * n + w]
        for at in range(0, hidden, step):
            here, there = slice(at, at + step), slice(hidden + at, hidden + at + step)
            gate_pre, up_proj = added(refs[:n], here), added(refs[:n], there)
            d_hidden = added(refs[n : 2 * n], here)
            sigmoid_gate = 1.0 / (1.0 + jnp.exp(-gate_pre))
            out[:, here] = (
                d_hidden * up_proj * sigmoid_gate * (1.0 + gate_pre * (1.0 - sigmoid_gate))
            ).astype(BF16)
            out[:, there] = (d_hidden * gate_pre * sigmoid_gate).astype(BF16)

    shapes, aliases = through(held, 2 * n, 1)
    results = pl.pallas_call(
        kernel,
        out_shape=[pltpu.VMEM((share, columns), BF16)] + shapes,
        in_specs=[IN_VMEM] * (2 * n + w),
        out_specs=[IN_VMEM] * (1 + w),
        input_output_aliases=aliases,
        compiler_params=params(4),
        name="gate_grads",
    )(*terms, *back_terms, *[in_vmem(a) for a in held])
    return results[0], results[1:]


def lay(place_ref, share_refs, laid):
    share = share_refs[0].shape[0]
    for j, ref in enumerate(share_refs):
        at = pl.multiple_of((place_ref[0] ^ j) * share, share)
        laid[pl.ds(at, share), :] = ref[...]


def output_terms(place, shares, down, held):
    groups, w = len(shares), len(held)
    total = shares[0].shape[0] * groups
    hidden, features = down.shape

    def kernel(place_ref, *refs):
        laid, out = refs[groups + 1 + w : groups + 3 + w]
        lay(place_ref, refs[:groups], laid)
        out[...] = jnp.dot(laid[...], refs[groups][...], preferred_element_type=F32)

    shapes, aliases = through(held, groups + 2, 2)
    results = pl.pallas_call(
        kernel,
        out_shape=[pltpu.VMEM((total, hidden), BF16), pltpu.VMEM((total, features), F32)] + shapes,
        in_specs=[IN_SMEM] + [IN_VMEM] * (groups + 1 + w),
        out_specs=[IN_VMEM] * (2 + w),
        input_output_aliases=aliases,
        compiler_params=params(4),
        name="output_terms",
    )(place, *shares, in_vmem(down), *[in_vmem(a) for a in held])
    return results[0], results[1], results[2:]


def input_terms(place, shares, gate, up, out_terms, own_rows):
    groups = len(shares)
    total = shares[0].shape[0] * groups
    features, hidden = gate.shape
    parts = total // own_rows

    def kernel(place_ref, *refs):
        gate_ref, up_ref, out_ref, laid, keep, send = refs[groups:]
        lay(place_ref, refs[:groups], laid)
        back = contract_cols(laid[:, :hidden], gate_ref[...])
        back = back + contract_cols(laid[:, hidden:], up_ref[...])
        for b in range(parts):
            rows = slice(b * own_rows, (b + 1) * own_rows)
            both = jnp.concatenate([out_ref[rows, :], back[rows]], axis=0)
            if b % 2:
                send[b // 2] = both.astype(BF16)
            else:
                keep[b // 2] = both

    shape = (parts // 2, 2 * own_rows, features)
    return pl.pallas_call(
        kernel,
        out_shape=[
            pltpu.VMEM((total, 2 * hidden), BF16),
            pltpu.VMEM(shape, F32),
            pltpu.VMEM(shape, BF16),
        ],
        in_specs=[IN_SMEM] + [IN_VMEM] * (groups + 3),
        out_specs=[IN_VMEM] * 3,
        compiler_params=params(4),
        name="input_terms",
    )(place, *shares, in_vmem(gate), in_vmem(up), out_terms)


def row_sum(keep, near, after):
    n = keep.shape[0]

    def kernel(keep_ref, near_ref, *refs):
        refs = refs[len(after) :]
        refs[0][...] = keep_ref[0] + near_ref[0].astype(F32)
        for j in range(1, n):
            refs[j][...] = (keep_ref[j] + near_ref[j].astype(F32)).astype(BF16)

    shape = keep.shape[1:]
    results = pl.pallas_call(
        kernel,
        out_shape=[pltpu.VMEM(shape, F32)] + [pltpu.VMEM(shape, BF16)] * (n - 1),
        in_specs=[IN_VMEM] * 2 + [ANYWHERE] * len(after),
        out_specs=[IN_VMEM] * n,
        compiler_params=params(4),
        name="row_sum",
    )(keep, near, *[in_hbm(a) for a in after])
    return results[0], results[1:]


def last_sum(total, far, after):
    n = len(far)
    both, features = total.shape

    def kernel(total_ref, *refs):
        outs = refs[n + len(after) :]
        value = total_ref[...]
        for ref in refs[:n]:
            value = value + ref[...].astype(F32)
        outs[0][...] = value[: both // 2].astype(BF16)
        outs[1][...] = value[both // 2 :].astype(BF16)

    return pl.pallas_call(
        kernel,
        out_shape=[jax.ShapeDtypeStruct((both // 2, features), BF16)] * 2,
        in_specs=[IN_VMEM] * (1 + n) + [ANYWHERE] * len(after),
        out_specs=[IN_VMEM] * 2,
        compiler_params=params(4),
        name="last_sum",
    )(total, *far, *[in_hbm(a) for a in after])


def outer(left, right, first, columns, held=(), after=()):
    rows = left.shape[1]
    w = len(held)
    tile = tile_of(rows, 256 if held else 256)
    slots = min(3 if held else 4, rows // tile)
    step = tile_of(columns, 512)

    def kernel(left_ref, right_ref, *refs):
        out, stage, sems = refs[w + len(after)], refs[-2], refs[-1]

        def sent(slot, at):
            return pltpu.make_async_copy(stage.at[slot], out.at[pl.ds(at, tile)], sems.at[slot])

        @pl.loop(0, rows // tile)
        def _(i):
            slot = lax.rem(i, slots)

            @pl.when(i >= slots)
            def _():
                sent(slot, 0).wait()

            at = pl.multiple_of(i * tile, tile)
            part = left_ref[:, pl.ds(at, tile)]
            for s in range(0, columns, step):
                stage[slot, :, s : s + step] = contract_rows(
                    part, right_ref[:, first + s : first + s + step]
                ).astype(BF16)
            sent(slot, at).start()

        for slot in range(slots):
            sent(slot, 0).wait()

    shapes, aliases = through(held, 2, 1)
    results = pl.pallas_call(
        kernel,
        out_shape=[jax.ShapeDtypeStruct((rows, columns), BF16)] + shapes,
        in_specs=[IN_VMEM] * (2 + w) + [ANYWHERE] * len(after),
        out_specs=[ANYWHERE] + [IN_VMEM] * w,
        scratch_shapes=[
            pltpu.VMEM((slots, tile, columns), BF16),
            pltpu.SemaphoreType.DMA((slots,)),
        ],
        input_output_aliases=aliases,
        compiler_params=params(4 if held else 12),
        cost_estimate=cost(moved=rows * columns * 2),
        name="outer",
    )(left, right, *[in_vmem(a) for a in held], *after)
    return results[0], results[1:]


def per_device(tokens, grad_out, gate_weight, up_weight, down_weight):
    own_rows = tokens.shape[0]
    rows, cores, chips = (lax.axis_size(a) for a in ("row", "depth", "col"))
    hidden = gate_weight.shape[1]
    place = lax.axis_index("depth").astype(jnp.int32).reshape(1)

    own = pack(tokens, grad_out)
    pair = join(own, swap(own, "row", 1))
    blocks = [pair] + [swap(pair, "row", k) for k in range(2, rows, 2)]
    gate, _ = load(gate_weight, [], (pair,))
    up, (gate,) = load(up_weight, [gate])
    down, (gate, up,) = make_room(down_weight, [gate, up])
    tok_all, grad_all, held = unpack(blocks, [gate, up, down])

    def over_cores(parts):
        return [parts[0]] + [swap(parts[j], "depth", j) for j in range(1, cores)]

    def over_chips(sums):
        total, rounded = sums
        return [total] + [swap(rounded, "col", k) for k in range(1, chips)]

    parts, held = first_products(place, tok_all, held, [0, 1], 0, hidden, cores)
    sums, held = core_sum([over_cores(parts)], held)
    terms = over_chips(sums)
    parts, held = back_products(place, grad_all, down_weight, held, cores)
    acts, held = hidden_units(terms, held)
    shares = over_cores([acts] * cores)
    sums, (*held, down) = core_sum([over_cores(parts)], held)
    back_terms = over_chips(sums)
    hid_all, out_terms, held = output_terms(place, shares, down, held)
    grad_down, held = outer(hid_all, grad_all, 0, grad_all.shape[1], held)
    acts, (gate, up) = gate_grads(terms, back_terms, held)
    shares = over_cores([acts] * cores)
    d_all, keep, send = input_terms(place, shares, gate, up, out_terms, own_rows)

    near = swap(send, "row", 1)
    grad_gate, _ = outer(tok_all, d_all, 0, hidden, (), (send,))
    total, rounded = row_sum(keep, near, (grad_gate,))
    far = [swap(rounded[j - 1], "row", 2 * j) for j in range(1, rows // 2)]
    grad_up, _ = outer(tok_all, d_all, hidden, hidden, (), (total,))
    layer_out, grad_tokens = last_sum(total, far, (grad_up,))
    return layer_out, grad_tokens, grad_gate, grad_up, grad_down


def solution(mesh):
    acts = P("row", ("col", "depth"))
    wide = P(("col", "depth"), "row")
    return jax.shard_map(
        per_device,
        mesh=mesh,
        in_specs=(acts, acts, wide, wide, acts),
        out_specs=(acts, acts, wide, wide, acts),
        check_vma=False,
    )
```

```python
import functools

import jax
import jax.numpy as jnp
from jax import lax
from jax.experimental import pallas as pl
from jax.experimental.pallas import tpu as pltpu
from jax.sharding import PartitionSpec as P

BF16 = jnp.bfloat16
F32 = jnp.float32
IN_VMEM = pl.BlockSpec(memory_space=pltpu.VMEM)
IN_SMEM = pl.BlockSpec(memory_space=pltpu.SMEM)
ANYWHERE = pl.BlockSpec(memory_space=pl.ANY)
MIB = 1 << 20


def params(mib):
    return pltpu.CompilerParams(vmem_limit_bytes=mib * MIB)


def cost(flops=0, moved=0, exps=0):
    return pl.CostEstimate(flops=flops, bytes_accessed=moved, transcendentals=exps)


def in_vmem(array):
    return pltpu.with_memory_space_constraint(array, pltpu.VMEM)


def in_hbm(array):
    return pltpu.with_memory_space_constraint(array, pltpu.HBM)


def swap(array, axis, distance):
    size = lax.axis_size(axis)
    return lax.ppermute(array, axis, [(i, i ^ distance) for i in range(size)])


def tile_of(extent, largest):
    best = 128
    for tile in range(128, largest + 1, 128):
        if extent % tile == 0:
            best = tile
    return best


def contract_cols(left, right):
    return lax.dot_general(left, right, (((1,), (1,)), ((), ())), preferred_element_type=F32)


def contract_rows(left, right):
    return lax.dot_general(left, right, (((0,), (0,)), ((), ())), preferred_element_type=F32)


def through(arrays, first_input, first_output):
    shapes = [pltpu.VMEM(a.shape, a.dtype) for a in arrays]
    return shapes, {first_input + i: first_output + i for i in range(len(arrays))}


def make_room(weight, held):
    shapes, aliases = through(held, 0, 1)
    results = pl.pallas_call(
        lambda *refs: None,
        out_shape=[pltpu.VMEM(weight.shape, weight.dtype)] + shapes,
        in_specs=[IN_VMEM] * len(held),
        out_specs=[IN_VMEM] * (1 + len(held)),
        input_output_aliases=aliases,
        compiler_params=params(4),
        name="make_room",
    )(*[in_vmem(a) for a in held])
    return results[0], results[1:]


def load(weight, held, after=()):
    parts = 4
    step = weight.shape[0] // parts

    def kernel(src, *refs):
        dst, sem = refs[len(held) + len(after)], refs[-1]
        copies = []
        for i in range(parts):
            rows = pl.ds(i * step, step)
            copies.append(pltpu.make_async_copy(src.at[rows], dst.at[rows], sem.at[i]))
            copies[-1].start()
        for copy in copies:
            copy.wait()

    shapes, aliases = through(held, 1, 1)
    results = pl.pallas_call(
        kernel,
        out_shape=[pltpu.VMEM(weight.shape, weight.dtype)] + shapes,
        in_specs=[ANYWHERE] + [IN_VMEM] * len(held) + [ANYWHERE] * len(after),
        out_specs=[IN_VMEM] * (1 + len(held)),
        scratch_shapes=[pltpu.SemaphoreType.DMA((parts,))],
        input_output_aliases=aliases,
        compiler_params=params(4),
        cost_estimate=cost(moved=weight.size * 2),
        name="load_weight",
    )(in_hbm(weight), *[in_vmem(a) for a in held], *after)
    return results[0], results[1:]


def pack(tokens, grad_out):
    own_rows, features = tokens.shape

    def kernel(tok_ref, grad_ref, out, stage, sems):
        copies = [
            pltpu.make_async_copy(ref, stage.at[i], sems.at[i])
            for i, ref in enumerate((tok_ref, grad_ref))
        ]
        for copy in copies:
            copy.start()
        for copy in copies:
            copy.wait()
        both = [stage[0].astype(F32), stage[1].astype(F32)]
        out[...] = jnp.concatenate(both, axis=0).astype(BF16)

    return pl.pallas_call(
        kernel,
        out_shape=pltpu.VMEM((2 * own_rows, features), BF16),
        in_specs=[ANYWHERE] * 2,
        out_specs=IN_VMEM,
        scratch_shapes=[
            pltpu.VMEM((2, own_rows, features), BF16),
            pltpu.SemaphoreType.DMA((2,)),
        ],
        compiler_params=params(4),
        name="pack",
    )(in_hbm(tokens), in_hbm(grad_out))


def join(own, near):
    both, features = own.shape
    own_rows = both // 2

    def kernel(own_ref, near_ref, out):
        pair = [own_ref[...].astype(F32), near_ref[...].astype(F32)]
        for g in range(2):
            half = slice(g * own_rows, (g + 1) * own_rows)
            out[g * both : (g + 1) * both, :] = jnp.concatenate(
                [p[half] for p in pair], axis=0
            ).astype(BF16)

    return pl.pallas_call(
        kernel,
        out_shape=pltpu.VMEM((2 * both, features), BF16),
        in_specs=[IN_VMEM] * 2,
        out_specs=IN_VMEM,
        compiler_params=params(4),
        name="join",
    )(own, near)


def unpack(blocks, held):
    n, w = len(blocks), len(held)
    rows, features = blocks[0].shape
    half = rows // 2

    def kernel(*refs):
        for b in range(n):
            for g in range(2):
                refs[n + w + g][b * half : (b + 1) * half, :] = refs[b][g * half : (g + 1) * half, :]

    shapes, aliases = through(held, n, 2)
    results = pl.pallas_call(
        kernel,
        out_shape=[pltpu.VMEM((n * half, features), BF16)] * 2 + shapes,
        in_specs=[IN_VMEM] * (n + w),
        out_specs=[IN_VMEM] * (2 + w),
        input_output_aliases=aliases,
        compiler_params=params(4),
        name="unpack",
    )(*blocks, *[in_vmem(a) for a in held])
    return results[0], results[1], results[2:]


def back_products(place, x, source, weights, groups):
    total = x.shape[0]
    share = total // groups
    hidden = source.shape[0]
    tile = tile_of(hidden, 1024)
    n, w = hidden // tile, len(weights)

    def kernel(place_ref, x_ref, src, *refs):
        outs, dst, acc, sems = refs[w : w + groups], refs[2 * w + groups - 1], refs[-2], refs[-1]
        spans = [slice(b * tile, (b + 1) * tile) for b in range(n)]
        copies = [
            pltpu.make_async_copy(src.at[spans[b]], dst.at[spans[b]], sems.at[b]) for b in range(n)
        ]
        for copy in copies:
            copy.start()
        for b in range(n):
            copies[b].wait()
            acc[...] = contract_cols(x_ref[...], dst[spans[b], :])
            for j in range(groups):
                at = pl.multiple_of((place_ref[0] ^ j) * share, share)
                outs[j][:, spans[b]] = acc[pl.ds(at, share), :]

    shapes, aliases = through(weights, 3, groups)
    results = pl.pallas_call(
        kernel,
        out_shape=[pltpu.VMEM((share, hidden), F32)] * groups + shapes,
        in_specs=[IN_SMEM, IN_VMEM, ANYWHERE] + [IN_VMEM] * w,
        out_specs=[IN_VMEM] * (groups + w),
        scratch_shapes=[pltpu.VMEM((total, tile), F32), pltpu.SemaphoreType.DMA((n,))],
        input_output_aliases=aliases,
        compiler_params=params(4),
        name="back_products",
    )(place, x, in_hbm(source), *[in_vmem(a) for a in weights])
    return results[:groups], results[groups:]


def first_products(place, x, weights, used, offset, width, groups):
    total = x.shape[0]
    share = total // groups
    n, w = len(used), len(weights)

    def kernel(place_ref, x_ref, *refs):
        outs, acc = refs[w : w + groups], refs[-1]
        for g in range(n):
            acc[...] = jnp.dot(
                x_ref[...],
                refs[used[g]][:, offset : offset + width],
                preferred_element_type=F32,
            )
            for j in range(groups):
                at = pl.multiple_of((place_ref[0] ^ j) * share, share)
                outs[j][:, g * width : (g + 1) * width] = acc[pl.ds(at, share), :]

    shapes, aliases = through(weights, 2, groups)
    results = pl.pallas_call(
        kernel,
        out_shape=[pltpu.VMEM((share, n * width), F32)] * groups + shapes,
        in_specs=[IN_SMEM] + [IN_VMEM] * (1 + w),
        out_specs=[IN_VMEM] * (groups + w),
        scratch_shapes=[pltpu.VMEM((total, width), F32)],
        input_output_aliases=aliases,
        compiler_params=params(4),
        name="first_products",
    )(place, x, *[in_vmem(a) for a in weights])
    return results[:groups], results[groups:]


def core_sum(pieces, weights):
    widths = [parts[0].shape[1] for parts in pieces]
    share, columns = pieces[0][0].shape[0], sum(widths)
    flat = [part for parts in pieces for part in parts]
    n, w, groups = len(flat), len(weights), len(pieces[0])

    def kernel(*refs):
        at = 0
        for p, width in enumerate(widths):
            total = refs[p * groups][...]
            for ref in refs[p * groups + 1 : (p + 1) * groups]:
                total = total + ref[...]
            refs[n + w][:, at : at + width] = total
            refs[n + w + 1][:, at : at + width] = total.astype(BF16)
            at += width

    shapes, aliases = through(weights, n, 2)
    results = pl.pallas_call(
        kernel,
        out_shape=[pltpu.VMEM((share, columns), F32), pltpu.VMEM((share, columns), BF16)] + shapes,
        in_specs=[IN_VMEM] * (n + w),
        out_specs=[IN_VMEM] * (2 + w),
        input_output_aliases=aliases,
        compiler_params=params(4),
        name="core_sum",
    )(*flat, *[in_vmem(a) for a in weights])
    return results[:2], results[2:]


def added(refs, cols):
    total = refs[0][:, cols]
    for ref in refs[1:]:
        total = total + ref[:, cols].astype(F32)
    return total


def hidden_units(terms, held):
    n, w = len(terms), len(held)
    share, columns = terms[0].shape
    hidden = columns // 2
    step = tile_of(hidden, 512)

    def kernel(*refs):
        for at in range(0, hidden, step):
            gate_pre = added(refs[:n], slice(at, at + step))
            up_proj = added(refs[:n], slice(hidden + at, hidden + at + step))
            sigmoid_gate = 1.0 / (1.0 + jnp.exp(-gate_pre))
            refs[n + w][:, at : at + step] = (gate_pre * sigmoid_gate * up_proj).astype(BF16)

    shapes, aliases = through(held, n, 1)
    results = pl.pallas_call(
        kernel,
        out_shape=[pltpu.VMEM((share, hidden), BF16)] + shapes,
        in_specs=[IN_VMEM] * (n + w),
        out_specs=[IN_VMEM] * (1 + w),
        input_output_aliases=aliases,
        compiler_params=params(4),
        name="hidden_units",
    )(*terms, *[in_vmem(a) for a in held])
    return results[0], results[1:]


def gate_grads(terms, back_terms, held):
    n, w = len(terms), len(held)
    share, columns = terms[0].shape
    hidden = columns // 2
    step = tile_of(hidden, 512)

    def kernel(*refs):
        out = refs[2 * n + w]
        for at in range(0, hidden, step):
            here, there = slice(at, at + step), slice(hidden + at, hidden + at + step)
            gate_pre, up_proj = added(refs[:n], here), added(refs[:n], there)
            d_hidden = added(refs[n : 2 * n], here)
            sigmoid_gate = 1.0 / (1.0 + jnp.exp(-gate_pre))
            out[:, here] = (
                d_hidden * up_proj * sigmoid_gate * (1.0 + gate_pre * (1.0 - sigmoid_gate))
            ).astype(BF16)
            out[:, there] = (d_hidden * gate_pre * sigmoid_gate).astype(BF16)

    shapes, aliases = through(held, 2 * n, 1)
    results = pl.pallas_call(
        kernel,
        out_shape=[pltpu.VMEM((share, columns), BF16)] + shapes,
        in_specs=[IN_VMEM] * (2 * n + w),
        out_specs=[IN_VMEM] * (1 + w),
        input_output_aliases=aliases,
        compiler_params=params(4),
        name="gate_grads",
    )(*terms, *back_terms, *[in_vmem(a) for a in held])
    return results[0], results[1:]


def lay(place_ref, share_refs, laid):
    share = share_refs[0].shape[0]
    for j, ref in enumerate(share_refs):
        at = pl.multiple_of((place_ref[0] ^ j) * share, share)
        laid[pl.ds(at, share), :] = ref[...]


def output_terms(place, shares, grad_all, down, held):
    groups, w = len(shares), len(held)
    total = shares[0].shape[0] * groups
    hidden, features = down.shape
    tile = tile_of(hidden, 512)
    n = hidden // tile
    step = tile_of(features, 512)

    def kernel(place_ref, *refs):
        grad_ref = refs[groups]
        out, grad_down, block = refs[groups + 2 + w : groups + 5 + w]
        laid, sems = refs[-2:]
        lay(place_ref, refs[:groups], laid)
        copies = []
        for i in range(n):
            rows = slice(i * tile, (i + 1) * tile)
            term = jnp.dot(laid[:, rows], block[rows, :], preferred_element_type=F32)
            out[...] = out[...] + term if i else term
            for at in range(0, features, step):
                block[rows, at : at + step] = contract_rows(
                    laid[:, rows], grad_ref[:, at : at + step]
                ).astype(BF16)
            copies.append(pltpu.make_async_copy(block.at[rows], grad_down.at[rows], sems.at[i]))
            copies[-1].start()
        for copy in copies:
            copy.wait()

    shapes, aliases = through([down, *held], groups + 2, 2)
    results = pl.pallas_call(
        kernel,
        out_shape=[
            pltpu.VMEM((total, features), F32),
            jax.ShapeDtypeStruct((hidden, features), BF16),
        ]
        + shapes,
        in_specs=[IN_SMEM] + [IN_VMEM] * (groups + 2 + w),
        out_specs=[IN_VMEM, ANYWHERE] + [IN_VMEM] * (1 + w),
        scratch_shapes=[pltpu.VMEM((total, hidden), BF16), pltpu.SemaphoreType.DMA((n,))],
        input_output_aliases=aliases,
        compiler_params=params(4),
        name="output_terms",
    )(place, *shares, grad_all, in_vmem(down), *[in_vmem(a) for a in held])
    return results[0], results[1], results[3:]


def input_terms(place, shares, gate, up, out_terms, own_rows):
    groups = len(shares)
    total = shares[0].shape[0] * groups
    features, hidden = gate.shape
    parts = total // own_rows
    tile = tile_of(features, 1024)

    def kernel(place_ref, *refs):
        gate_ref, up_ref, out_ref, laid, keep, send = refs[groups:]
        lay(place_ref, refs[:groups], laid)
        d_gate, d_up = laid[:, :hidden].T, laid[:, hidden:].T
        for at in range(0, features, tile):
            cols = slice(at, at + tile)
            back = jnp.dot(gate_ref[cols, :], d_gate, preferred_element_type=F32)
            back = back + jnp.dot(up_ref[cols, :], d_up, preferred_element_type=F32)
            back = back.T
            for b in range(parts):
                rows = slice(b * own_rows, (b + 1) * own_rows)
                both = jnp.concatenate([out_ref[rows, cols], back[rows]], axis=0)
                if b % 2:
                    send[b // 2, :, cols] = both.astype(BF16)
                else:
                    keep[b // 2, :, cols] = both

    shape = (parts // 2, 2 * own_rows, features)
    return pl.pallas_call(
        kernel,
        out_shape=[
            pltpu.VMEM((total, 2 * hidden), BF16),
            pltpu.VMEM(shape, F32),
            pltpu.VMEM(shape, BF16),
        ],
        in_specs=[IN_SMEM] + [IN_VMEM] * (groups + 3),
        out_specs=[IN_VMEM] * 3,
        compiler_params=params(4),
        name="input_terms",
    )(place, *shares, in_vmem(gate), in_vmem(up), out_terms)


def row_sum(keep, near, after):
    n = keep.shape[0]

    def kernel(keep_ref, near_ref, *refs):
        refs = refs[len(after) :]
        refs[0][...] = keep_ref[0] + near_ref[0].astype(F32)
        for j in range(1, n):
            refs[j][...] = (keep_ref[j] + near_ref[j].astype(F32)).astype(BF16)

    shape = keep.shape[1:]
    results = pl.pallas_call(
        kernel,
        out_shape=[pltpu.VMEM(shape, F32)] + [pltpu.VMEM(shape, BF16)] * (n - 1),
        in_specs=[IN_VMEM] * 2 + [ANYWHERE] * len(after),
        out_specs=[IN_VMEM] * n,
        compiler_params=params(4),
        name="row_sum",
    )(keep, near, *[in_hbm(a) for a in after])
    return results[0], results[1:]


def last_sum(total, far, after):
    n = len(far)
    both, features = total.shape

    def kernel(total_ref, *refs):
        outs = refs[n + len(after) :]
        value = total_ref[...]
        for ref in refs[:n]:
            value = value + ref[...].astype(F32)
        outs[0][...] = value[: both // 2].astype(BF16)
        outs[1][...] = value[both // 2 :].astype(BF16)

    return pl.pallas_call(
        kernel,
        out_shape=[jax.ShapeDtypeStruct((both // 2, features), BF16)] * 2,
        in_specs=[IN_VMEM] * (1 + n) + [ANYWHERE] * len(after),
        out_specs=[IN_VMEM] * 2,
        compiler_params=params(4),
        name="last_sum",
    )(total, *far, *[in_hbm(a) for a in after])


def outer_here(left, right, first, columns, after):
    rows = left.shape[1]
    step = tile_of(columns, 256)

    def kernel(left_ref, right_ref, *refs):
        out = refs[len(after)]

        @pl.loop(0, columns // step)
        def _(i):
            at = pl.multiple_of(i * step, step)
            out[:, pl.ds(at, step)] = contract_rows(
                left_ref[...], right_ref[:, pl.ds(first + at, step)]
            ).astype(BF16)

    return pl.pallas_call(
        kernel,
        out_shape=pltpu.VMEM((rows, columns), BF16),
        in_specs=[IN_VMEM] * 2 + [ANYWHERE] * len(after),
        out_specs=IN_VMEM,
        compiler_params=params(8),
        cost_estimate=cost(moved=rows * columns * 2),
        name="outer_here",
    )(left, right, *after)


def outer(left, right, first, columns, after):
    rows = left.shape[1]
    step = tile_of(columns, 512)
    blocks, at = [], 0
    for size in (128, 128, 256):
        if at + size < rows:
            blocks.append((at, size))
            at += size
    while at < rows:
        size = min(512, rows - at)
        blocks.append((at, size))
        at += size

    def kernel(left_ref, right_ref, *refs):
        out, stage, sems = refs[len(after) :]
        copies = []
        for i, (at, size) in enumerate(blocks):
            block = slice(at, at + size)
            for s in range(0, columns, step):
                stage[block, s : s + step] = contract_rows(
                    left_ref[:, block], right_ref[:, first + s : first + s + step]
                ).astype(BF16)
            copies.append(pltpu.make_async_copy(stage.at[block], out.at[block], sems.at[i]))
            copies[-1].start()
        for copy in copies:
            copy.wait()

    return pl.pallas_call(
        kernel,
        out_shape=jax.ShapeDtypeStruct((rows, columns), BF16),
        in_specs=[IN_VMEM] * 2 + [ANYWHERE] * len(after),
        out_specs=ANYWHERE,
        scratch_shapes=[
            pltpu.VMEM((rows, columns), BF16),
            pltpu.SemaphoreType.DMA((len(blocks),)),
        ],
        compiler_params=params(20),
        cost_estimate=cost(moved=rows * columns * 2),
        name="outer",
    )(left, right, *after)


def per_device(tokens, grad_out, gate_weight, up_weight, down_weight):
    own_rows = tokens.shape[0]
    rows, cores, chips = (lax.axis_size(a) for a in ("row", "depth", "col"))
    hidden = gate_weight.shape[1]
    place = lax.axis_index("depth").astype(jnp.int32).reshape(1)

    own = pack(tokens, grad_out)
    pair = join(own, swap(own, "row", 1))
    blocks = [pair] + [swap(pair, "row", k) for k in range(2, rows, 2)]
    gate, _ = load(gate_weight, [], (pair,))
    up, (gate,) = load(up_weight, [gate])
    down, (gate, up,) = make_room(down_weight, [gate, up])
    tok_all, grad_all, held = unpack(blocks, [gate, up, down])

    def over_cores(parts):
        return [parts[0]] + [swap(parts[j], "depth", j) for j in range(1, cores)]

    def over_chips(sums):
        total, rounded = sums
        return [total] + [swap(rounded, "col", k) for k in range(1, chips)]

    pieces = []
    for which in (0, 1):
        parts, held = first_products(place, tok_all, held, [which], 0, hidden, cores)
        pieces.append(over_cores(parts))
    sums, held = core_sum(pieces, held)
    terms = over_chips(sums)
    parts, held = back_products(place, grad_all, down_weight, held, cores)
    acts, held = hidden_units(terms, held)
    shares = over_cores([acts] * cores)
    sums, (*held, down) = core_sum([over_cores(parts)], held)
    back_terms = over_chips(sums)
    out_terms, grad_down, held = output_terms(place, shares, grad_all, down, held)
    acts, (gate, up) = gate_grads(terms, back_terms, held)
    shares = over_cores([acts] * cores)
    d_all, keep, send = input_terms(place, shares, gate, up, out_terms, own_rows)

    near = swap(send, "row", 1)
    grad_gate = outer(tok_all, d_all, 0, hidden, (send,))
    total, rounded = row_sum(keep, near, (grad_gate,))
    far = [swap(rounded[j - 1], "row", 2 * j) for j in range(1, rows // 2)]
    grad_up = outer(tok_all, d_all, hidden, hidden, (total,))
    layer_out, grad_tokens = last_sum(total, far, (grad_up,))
    return layer_out, grad_tokens, grad_gate, grad_up, grad_down


def solution(mesh):
    acts = P("row", ("col", "depth"))
    wide = P(("col", "depth"), "row")
    return jax.shard_map(
        per_device,
        mesh=mesh,
        in_specs=(acts, acts, wide, wide, acts),
        out_specs=(acts, acts, wide, wide, acts),
        check_vma=False,
    )
```

```python
import functools

import jax
import jax.numpy as jnp
from jax import lax
from jax.experimental import pallas as pl
from jax.experimental.pallas import tpu as pltpu
from jax.sharding import PartitionSpec as P

BF16 = jnp.bfloat16
F32 = jnp.float32
IN_VMEM = pl.BlockSpec(memory_space=pltpu.VMEM)
IN_SMEM = pl.BlockSpec(memory_space=pltpu.SMEM)
ANYWHERE = pl.BlockSpec(memory_space=pl.ANY)
MIB = 1 << 20


def params(mib):
    return pltpu.CompilerParams(vmem_limit_bytes=mib * MIB)


def cost(flops=0, moved=0, exps=0):
    return pl.CostEstimate(flops=flops, bytes_accessed=moved, transcendentals=exps)


def in_vmem(array):
    return pltpu.with_memory_space_constraint(array, pltpu.VMEM)


def in_hbm(array):
    return pltpu.with_memory_space_constraint(array, pltpu.HBM)


def swap(array, axis, distance):
    size = lax.axis_size(axis)
    return lax.ppermute(array, axis, [(i, i ^ distance) for i in range(size)])


def tile_of(extent, largest):
    best = 128
    for tile in range(128, largest + 1, 128):
        if extent % tile == 0:
            best = tile
    return best


def contract_cols(left, right):
    return lax.dot_general(left, right, (((1,), (1,)), ((), ())), preferred_element_type=F32)


def contract_rows(left, right):
    return lax.dot_general(left, right, (((0,), (0,)), ((), ())), preferred_element_type=F32)


def through(arrays, first_input, first_output):
    shapes = [pltpu.VMEM(a.shape, a.dtype) for a in arrays]
    return shapes, {first_input + i: first_output + i for i in range(len(arrays))}


def make_room(weight, held):
    shapes, aliases = through(held, 0, 1)
    results = pl.pallas_call(
        lambda *refs: None,
        out_shape=[pltpu.VMEM(weight.shape, weight.dtype)] + shapes,
        in_specs=[IN_VMEM] * len(held),
        out_specs=[IN_VMEM] * (1 + len(held)),
        input_output_aliases=aliases,
        compiler_params=params(4),
        name="make_room",
    )(*[in_vmem(a) for a in held])
    return results[0], results[1:]


def load(weight, held, after=(), share=1):
    parts = 4
    step = weight.shape[0] // (share * parts)

    def kernel(src, *refs):
        dst, sem = refs[len(held) + len(after)], refs[-1]
        copies = []
        for i in range(parts):
            rows = pl.ds(i * step, step)
            copies.append(pltpu.make_async_copy(src.at[rows], dst.at[rows], sem.at[i]))
            copies[-1].start()
        for copy in copies:
            copy.wait()

    shapes, aliases = through(held, 1, 1)
    results = pl.pallas_call(
        kernel,
        out_shape=[pltpu.VMEM(weight.shape, weight.dtype)] + shapes,
        in_specs=[ANYWHERE] + [IN_VMEM] * len(held) + [ANYWHERE] * len(after),
        out_specs=[IN_VMEM] * (1 + len(held)),
        scratch_shapes=[pltpu.SemaphoreType.DMA((parts,))],
        input_output_aliases=aliases,
        compiler_params=params(4),
        cost_estimate=cost(moved=weight.size * 2),
        name="load_weight",
    )(in_hbm(weight), *[in_vmem(a) for a in held], *after)
    return results[0], results[1:]


def pack(tokens, grad_out):
    own_rows, features = tokens.shape

    def kernel(tok_ref, grad_ref, out, stage, sems):
        copies = [
            pltpu.make_async_copy(ref, stage.at[i], sems.at[i])
            for i, ref in enumerate((tok_ref, grad_ref))
        ]
        for copy in copies:
            copy.start()
        for copy in copies:
            copy.wait()
        both = [stage[0].astype(F32), stage[1].astype(F32)]
        out[...] = jnp.concatenate(both, axis=0).astype(BF16)

    return pl.pallas_call(
        kernel,
        out_shape=pltpu.VMEM((2 * own_rows, features), BF16),
        in_specs=[ANYWHERE] * 2,
        out_specs=IN_VMEM,
        scratch_shapes=[
            pltpu.VMEM((2, own_rows, features), BF16),
            pltpu.SemaphoreType.DMA((2,)),
        ],
        compiler_params=params(4),
        name="pack",
    )(in_hbm(tokens), in_hbm(grad_out))


def join(own, near):
    both, features = own.shape
    own_rows = both // 2

    def kernel(own_ref, near_ref, out):
        pair = [own_ref[...].astype(F32), near_ref[...].astype(F32)]
        for g in range(2):
            half = slice(g * own_rows, (g + 1) * own_rows)
            out[g * both : (g + 1) * both, :] = jnp.concatenate(
                [p[half] for p in pair], axis=0
            ).astype(BF16)

    return pl.pallas_call(
        kernel,
        out_shape=pltpu.VMEM((2 * both, features), BF16),
        in_specs=[IN_VMEM] * 2,
        out_specs=IN_VMEM,
        compiler_params=params(4),
        name="join",
    )(own, near)


def unpack(blocks, held):
    n, w = len(blocks), len(held)
    rows, features = blocks[0].shape
    half = rows // 2

    def kernel(*refs):
        for b in range(n):
            for g in range(2):
                refs[n + w + g][b * half : (b + 1) * half, :] = refs[b][g * half : (g + 1) * half, :]

    shapes, aliases = through(held, n, 2)
    results = pl.pallas_call(
        kernel,
        out_shape=[pltpu.VMEM((n * half, features), BF16)] * 2 + shapes,
        in_specs=[IN_VMEM] * (n + w),
        out_specs=[IN_VMEM] * (2 + w),
        input_output_aliases=aliases,
        compiler_params=params(4),
        name="unpack",
    )(*blocks, *[in_vmem(a) for a in held])
    return results[0], results[1], results[2:]


def back_products(place, x, source, weights, groups):
    total = x.shape[0]
    share = total // groups
    hidden = source.shape[0]
    tile = tile_of(hidden, 1024)
    n, w = hidden // tile, len(weights)

    def kernel(place_ref, x_ref, src, *refs):
        outs, dst = refs[w : w + groups * n], refs[2 * w + groups * n - 1]
        acc, sems = refs[-2:]
        spans = [slice(b * tile, (b + 1) * tile) for b in range(n)]
        copies = [
            pltpu.make_async_copy(src.at[spans[b]], dst.at[spans[b]], sems.at[b]) for b in range(n)
        ]
        for copy in copies:
            copy.start()
        for b in range(n):
            copies[b].wait()
            acc[...] = contract_cols(x_ref[...], dst[spans[b], :])
            for j in range(groups):
                at = pl.multiple_of((place_ref[0] ^ j) * share, share)
                outs[j * n + b][...] = acc[pl.ds(at, share), :]

    shapes, aliases = through(weights, 3, groups * n)
    results = pl.pallas_call(
        kernel,
        out_shape=[pltpu.VMEM((share, tile), F32)] * (groups * n) + shapes,
        in_specs=[IN_SMEM, IN_VMEM, ANYWHERE] + [IN_VMEM] * w,
        out_specs=[IN_VMEM] * (groups * n + w),
        scratch_shapes=[pltpu.VMEM((total, tile), F32), pltpu.SemaphoreType.DMA((n,))],
        input_output_aliases=aliases,
        compiler_params=params(4),
        name="back_products",
    )(place, x, in_hbm(source), *[in_vmem(a) for a in weights])
    return [results[b : groups * n : n] for b in range(n)], results[groups * n :]


def first_products(place, x, weights, used, offset, width, groups, rest=None):
    total = x.shape[0]
    source = () if rest is None else (rest[0],)
    share = total // groups
    n, w = len(used), len(weights)

    def kernel(place_ref, x_ref, *refs):
        acc, sems = refs[-2:]
        copies = []
        if source:
            dst = refs[1 + w + groups + rest[1]]
            first = dst.shape[0] // rest[2]
            step = (dst.shape[0] - first) // 4
            for i in range(4):
                rows = pl.ds(first + i * step, step)
                copies.append(pltpu.make_async_copy(refs[0].at[rows], dst.at[rows], sems.at[i]))
                copies[-1].start()
        refs = refs[len(source) :]
        outs = refs[w : w + groups]
        for g in range(n):
            acc[...] = jnp.dot(
                x_ref[...],
                refs[used[g]][:, offset : offset + width],
                preferred_element_type=F32,
            )
            for j in range(groups):
                at = pl.multiple_of((place_ref[0] ^ j) * share, share)
                outs[j][:, g * width : (g + 1) * width] = acc[pl.ds(at, share), :]
        for copy in copies:
            copy.wait()

    shapes, aliases = through(weights, 2 + len(source), groups)
    results = pl.pallas_call(
        kernel,
        out_shape=[pltpu.VMEM((share, n * width), F32)] * groups + shapes,
        in_specs=[IN_SMEM, IN_VMEM] + [ANYWHERE] * len(source) + [IN_VMEM] * w,
        out_specs=[IN_VMEM] * (groups + w),
        scratch_shapes=[pltpu.VMEM((total, width), F32), pltpu.SemaphoreType.DMA((4,))],
        input_output_aliases=aliases,
        compiler_params=params(4),
        name="first_products",
    )(place, x, *[in_hbm(a) for a in source], *[in_vmem(a) for a in weights])
    return results[:groups], results[groups:]


def core_sum(pieces, weights):
    widths = [parts[0].shape[1] for parts in pieces]
    share, columns = pieces[0][0].shape[0], sum(widths)
    flat = [part for parts in pieces for part in parts]
    n, w, groups = len(flat), len(weights), len(pieces[0])

    def kernel(*refs):
        at = 0
        for p, width in enumerate(widths):
            total = refs[p * groups][...]
            for ref in refs[p * groups + 1 : (p + 1) * groups]:
                total = total + ref[...]
            refs[n + w][:, at : at + width] = total
            refs[n + w + 1][:, at : at + width] = total.astype(BF16)
            at += width

    shapes, aliases = through(weights, n, 2)
    results = pl.pallas_call(
        kernel,
        out_shape=[pltpu.VMEM((share, columns), F32), pltpu.VMEM((share, columns), BF16)] + shapes,
        in_specs=[IN_VMEM] * (n + w),
        out_specs=[IN_VMEM] * (2 + w),
        input_output_aliases=aliases,
        compiler_params=params(4),
        name="core_sum",
    )(*flat, *[in_vmem(a) for a in weights])
    return results[:2], results[2:]


def added(refs, cols):
    total = refs[0][:, cols]
    for ref in refs[1:]:
        total = total + ref[:, cols].astype(F32)
    return total


def hidden_units(terms, held):
    n, w = len(terms[0]), len(held)
    share, hidden = terms[0][0].shape
    step = tile_of(hidden, 512)

    def kernel(*refs):
        for at in range(0, hidden, step):
            gate_pre = added(refs[:n], slice(at, at + step))
            up_proj = added(refs[n : 2 * n], slice(at, at + step))
            sigmoid_gate = 1.0 / (1.0 + jnp.exp(-gate_pre))
            refs[2 * n + w][:, at : at + step] = (gate_pre * sigmoid_gate * up_proj).astype(BF16)

    shapes, aliases = through(held, 2 * n, 1)
    results = pl.pallas_call(
        kernel,
        out_shape=[pltpu.VMEM((share, hidden), BF16)] + shapes,
        in_specs=[IN_VMEM] * (2 * n + w),
        out_specs=[IN_VMEM] * (1 + w),
        input_output_aliases=aliases,
        compiler_params=params(4),
        name="hidden_units",
    )(*terms[0], *terms[1], *[in_vmem(a) for a in held])
    return results[0], results[1:]


def gate_grads(terms, back_terms, held):
    n, w = len(back_terms), len(held)
    share, hidden = back_terms[0].shape
    columns = 2 * hidden
    step = tile_of(hidden, 512)

    def kernel(*refs):
        out = refs[3 * n + w]
        for at in range(0, hidden, step):
            here, there = slice(at, at + step), slice(hidden + at, hidden + at + step)
            gate_pre, up_proj = added(refs[:n], here), added(refs[n : 2 * n], here)
            d_hidden = added(refs[2 * n : 3 * n], here)
            sigmoid_gate = 1.0 / (1.0 + jnp.exp(-gate_pre))
            out[:, here] = (
                d_hidden * up_proj * sigmoid_gate * (1.0 + gate_pre * (1.0 - sigmoid_gate))
            ).astype(BF16)
            out[:, there] = (d_hidden * gate_pre * sigmoid_gate).astype(BF16)

    shapes, aliases = through(held, 3 * n, 1)
    results = pl.pallas_call(
        kernel,
        out_shape=[pltpu.VMEM((share, columns), BF16)] + shapes,
        in_specs=[IN_VMEM] * (3 * n + w),
        out_specs=[IN_VMEM] * (1 + w),
        input_output_aliases=aliases,
        compiler_params=params(4),
        name="gate_grads",
    )(*terms[0], *terms[1], *back_terms, *[in_vmem(a) for a in held])
    return results[0], results[1:]


def lay(place_ref, share_refs, laid):
    share = share_refs[0].shape[0]
    for j, ref in enumerate(share_refs):
        at = pl.multiple_of((place_ref[0] ^ j) * share, share)
        laid[pl.ds(at, share), :] = ref[...]


def output_terms(place, shares, grad_all, down, held):
    groups, w = len(shares), len(held)
    total = shares[0].shape[0] * groups
    hidden, features = down.shape
    tile = tile_of(hidden, 512)
    n = hidden // tile
    step = tile_of(features, 512)

    def kernel(place_ref, *refs):
        grad_ref = refs[groups]
        out, grad_down, block = refs[groups + 2 + w : groups + 5 + w]
        laid, sems = refs[-2:]
        lay(place_ref, refs[:groups], laid)
        copies = []
        for i in range(n):
            rows = slice(i * tile, (i + 1) * tile)
            term = jnp.dot(laid[:, rows], block[rows, :], preferred_element_type=F32)
            out[...] = out[...] + term if i else term
            for at in range(0, features, step):
                block[rows, at : at + step] = contract_rows(
                    laid[:, rows], grad_ref[:, at : at + step]
                ).astype(BF16)
            copies.append(pltpu.make_async_copy(block.at[rows], grad_down.at[rows], sems.at[i]))
            copies[-1].start()
        for copy in copies:
            copy.wait()

    shapes, aliases = through([down, *held], groups + 2, 2)
    results = pl.pallas_call(
        kernel,
        out_shape=[
            pltpu.VMEM((total, features), F32),
            jax.ShapeDtypeStruct((hidden, features), BF16),
        ]
        + shapes,
        in_specs=[IN_SMEM] + [IN_VMEM] * (groups + 2 + w),
        out_specs=[IN_VMEM, ANYWHERE] + [IN_VMEM] * (1 + w),
        scratch_shapes=[pltpu.VMEM((total, hidden), BF16), pltpu.SemaphoreType.DMA((n,))],
        input_output_aliases=aliases,
        compiler_params=params(4),
        name="output_terms",
    )(place, *shares, grad_all, in_vmem(down), *[in_vmem(a) for a in held])
    return results[0], results[1], results[3:]


def input_terms(place, shares, gate, up, out_terms, own_rows):
    groups = len(shares)
    total = shares[0].shape[0] * groups
    features, hidden = gate.shape
    parts = total // own_rows
    tile = tile_of(features, 1024)

    def kernel(place_ref, *refs):
        gate_ref, up_ref, out_ref, laid, keep, send = refs[groups:]
        lay(place_ref, refs[:groups], laid)
        d_gate, d_up = laid[:, :hidden].T, laid[:, hidden:].T
        for at in range(0, features, tile):
            cols = slice(at, at + tile)
            back = jnp.dot(gate_ref[cols, :], d_gate, preferred_element_type=F32)
            back = back + jnp.dot(up_ref[cols, :], d_up, preferred_element_type=F32)
            back = back.T
            for b in range(parts):
                rows = slice(b * own_rows, (b + 1) * own_rows)
                both = jnp.concatenate([out_ref[rows, cols], back[rows]], axis=0)
                if b % 2:
                    send[b // 2, :, cols] = both.astype(BF16)
                else:
                    keep[b // 2, :, cols] = both

    shape = (parts // 2, 2 * own_rows, features)
    return pl.pallas_call(
        kernel,
        out_shape=[
            pltpu.VMEM((total, 2 * hidden), BF16),
            pltpu.VMEM(shape, F32),
            pltpu.VMEM(shape, BF16),
        ],
        in_specs=[IN_SMEM] + [IN_VMEM] * (groups + 3),
        out_specs=[IN_VMEM] * 3,
        compiler_params=params(4),
        name="input_terms",
    )(place, *shares, in_vmem(gate), in_vmem(up), out_terms)


def row_sum(keep, near, after):
    n = keep.shape[0]

    def kernel(keep_ref, near_ref, *refs):
        refs = refs[len(after) :]
        refs[0][...] = keep_ref[0] + near_ref[0].astype(F32)
        for j in range(1, n):
            refs[j][...] = (keep_ref[j] + near_ref[j].astype(F32)).astype(BF16)

    shape = keep.shape[1:]
    results = pl.pallas_call(
        kernel,
        out_shape=[pltpu.VMEM(shape, F32)] + [pltpu.VMEM(shape, BF16)] * (n - 1),
        in_specs=[IN_VMEM] * 2 + [ANYWHERE] * len(after),
        out_specs=[IN_VMEM] * n,
        compiler_params=params(4),
        name="row_sum",
    )(keep, near, *[in_hbm(a) for a in after])
    return results[0], results[1:]


def last_sum(total, far, after):
    n = len(far)
    both, features = total.shape

    def kernel(total_ref, *refs):
        outs = refs[n + len(after) :]
        value = total_ref[...]
        for ref in refs[:n]:
            value = value + ref[...].astype(F32)
        outs[0][...] = value[: both // 2].astype(BF16)
        outs[1][...] = value[both // 2 :].astype(BF16)

    return pl.pallas_call(
        kernel,
        out_shape=[jax.ShapeDtypeStruct((both // 2, features), BF16)] * 2,
        in_specs=[IN_VMEM] * (1 + n) + [ANYWHERE] * len(after),
        out_specs=[IN_VMEM] * 2,
        compiler_params=params(4),
        name="last_sum",
    )(total, *far, *[in_hbm(a) for a in after])


def outer_here(left, right, first, columns, after):
    rows = left.shape[1]
    step = tile_of(columns, 256)

    def kernel(left_ref, right_ref, *refs):
        out = refs[len(after)]

        @pl.loop(0, columns // step)
        def _(i):
            at = pl.multiple_of(i * step, step)
            out[:, pl.ds(at, step)] = contract_rows(
                left_ref[...], right_ref[:, pl.ds(first + at, step)]
            ).astype(BF16)

    return pl.pallas_call(
        kernel,
        out_shape=pltpu.VMEM((rows, columns), BF16),
        in_specs=[IN_VMEM] * 2 + [ANYWHERE] * len(after),
        out_specs=IN_VMEM,
        compiler_params=params(8),
        cost_estimate=cost(moved=rows * columns * 2),
        name="outer_here",
    )(left, right, *after)


def outer(left, right, first, columns, after):
    rows = left.shape[1]
    step = tile_of(columns, 512)
    blocks, at = [], 0
    for size in (128, 128, 256):
        if at + size < rows:
            blocks.append((at, size))
            at += size
    while at < rows:
        size = min(512, rows - at)
        blocks.append((at, size))
        at += size

    def kernel(left_ref, right_ref, *refs):
        out, stage, sems = refs[len(after) :]
        copies = []
        for i, (at, size) in enumerate(blocks):
            block = slice(at, at + size)
            for s in range(0, columns, step):
                stage[block, s : s + step] = contract_rows(
                    left_ref[:, block], right_ref[:, first + s : first + s + step]
                ).astype(BF16)
            copies.append(pltpu.make_async_copy(stage.at[block], out.at[block], sems.at[i]))
            copies[-1].start()
        for copy in copies:
            copy.wait()

    return pl.pallas_call(
        kernel,
        out_shape=jax.ShapeDtypeStruct((rows, columns), BF16),
        in_specs=[IN_VMEM] * 2 + [ANYWHERE] * len(after),
        out_specs=ANYWHERE,
        scratch_shapes=[
            pltpu.VMEM((rows, columns), BF16),
            pltpu.SemaphoreType.DMA((len(blocks),)),
        ],
        compiler_params=params(20),
        cost_estimate=cost(moved=rows * columns * 2),
        name="outer",
    )(left, right, *after)


def per_device(tokens, grad_out, gate_weight, up_weight, down_weight):
    own_rows = tokens.shape[0]
    rows, cores, chips = (lax.axis_size(a) for a in ("row", "depth", "col"))
    hidden = gate_weight.shape[1]
    place = lax.axis_index("depth").astype(jnp.int32).reshape(1)

    own = pack(tokens, grad_out)
    pair = join(own, swap(own, "row", 1))
    blocks = [pair] + [swap(pair, "row", k) for k in range(2, rows, 2)]
    gate, _ = load(gate_weight, [], (pair,))
    up, (gate,) = load(up_weight, [gate], (), 2)
    down, (gate, up,) = make_room(down_weight, [gate, up])
    tok_all, grad_all, held = unpack(blocks, [gate, up, down])

    def over_cores(parts):
        return [parts[0]] + [swap(parts[j], "depth", j) for j in range(1, cores)]

    def over_chips(sums):
        total, rounded = sums
        return [total] + [swap(rounded, "col", k) for k in range(1, chips)]

    parted, terms = [], []
    for which in (0, 1):
        rest = None if which else (up_weight, 1, 2)
        parts, held = first_products(place, tok_all, held, [which], 0, hidden, cores, rest)
        parted.append(over_cores(parts))
    for parts in parted:
        sums, held = core_sum([parts], held)
        terms.append(over_chips(sums))
    back_parts, held = back_products(place, grad_all, down_weight, held, cores)
    back_parts = [over_cores(parts) for parts in back_parts]
    acts, held = hidden_units(terms, held)
    shares = over_cores([acts] * cores)
    sums, (*held, down) = core_sum(back_parts, held)
    back_terms = over_chips(sums)
    out_terms, grad_down, held = output_terms(place, shares, grad_all, down, held)
    acts, (gate, up) = gate_grads(terms, back_terms, held)
    shares = over_cores([acts] * cores)
    d_all, keep, send = input_terms(place, shares, gate, up, out_terms, own_rows)

    near = swap(send, "row", 1)
    grad_gate = outer(tok_all, d_all, 0, hidden, (send,))
    total, rounded = row_sum(keep, near, (grad_gate,))
    far = [swap(rounded[j - 1], "row", 2 * j) for j in range(1, rows // 2)]
    grad_up = outer(tok_all, d_all, hidden, hidden, (total,))
    layer_out, grad_tokens = last_sum(total, far, (grad_up,))
    return layer_out, grad_tokens, grad_gate, grad_up, grad_down


def solution(mesh):
    acts = P("row", ("col", "depth"))
    wide = P(("col", "depth"), "row")
    return jax.shard_map(
        per_device,
        mesh=mesh,
        in_specs=(acts, acts, wide, wide, acts),
        out_specs=(acts, acts, wide, wide, acts),
        check_vma=False,
    )
```

```python
import functools

import jax
import jax.numpy as jnp
from jax import lax
from jax.experimental import pallas as pl
from jax.experimental.pallas import tpu as pltpu
from jax.sharding import PartitionSpec as P

BF16 = jnp.bfloat16
F32 = jnp.float32
IN_VMEM = pl.BlockSpec(memory_space=pltpu.VMEM)
IN_SMEM = pl.BlockSpec(memory_space=pltpu.SMEM)
ANYWHERE = pl.BlockSpec(memory_space=pl.ANY)
MIB = 1 << 20


def params(mib):
    return pltpu.CompilerParams(vmem_limit_bytes=mib * MIB)


def cost(flops=0, moved=0, exps=0):
    return pl.CostEstimate(flops=flops, bytes_accessed=moved, transcendentals=exps)


def in_vmem(array):
    return pltpu.with_memory_space_constraint(array, pltpu.VMEM)


def in_hbm(array):
    return pltpu.with_memory_space_constraint(array, pltpu.HBM)


def swap(array, axis, distance):
    size = lax.axis_size(axis)
    return lax.ppermute(array, axis, [(i, i ^ distance) for i in range(size)])


def tile_of(extent, largest):
    best = 128
    for tile in range(128, largest + 1, 128):
        if extent % tile == 0:
            best = tile
    return best


def contract_cols(left, right):
    return lax.dot_general(left, right, (((1,), (1,)), ((), ())), preferred_element_type=F32)


def contract_rows(left, right):
    return lax.dot_general(left, right, (((0,), (0,)), ((), ())), preferred_element_type=F32)


def through(arrays, first_input, first_output):
    shapes = [pltpu.VMEM(a.shape, a.dtype) for a in arrays]
    return shapes, {first_input + i: first_output + i for i in range(len(arrays))}


def make_room(weight, held):
    shapes, aliases = through(held, 0, 1)
    results = pl.pallas_call(
        lambda *refs: None,
        out_shape=[pltpu.VMEM(weight.shape, weight.dtype)] + shapes,
        in_specs=[IN_VMEM] * len(held),
        out_specs=[IN_VMEM] * (1 + len(held)),
        input_output_aliases=aliases,
        compiler_params=params(4),
        name="make_room",
    )(*[in_vmem(a) for a in held])
    return results[0], results[1:]


def load(weight, held, after=(), share=1):
    parts = 4
    step = weight.shape[0] // (share * parts)

    def kernel(src, *refs):
        dst, sem = refs[len(held) + len(after)], refs[-1]
        copies = []
        for i in range(parts):
            rows = pl.ds(i * step, step)
            copies.append(pltpu.make_async_copy(src.at[rows], dst.at[rows], sem.at[i]))
            copies[-1].start()
        for copy in copies:
            copy.wait()

    shapes, aliases = through(held, 1, 1)
    results = pl.pallas_call(
        kernel,
        out_shape=[pltpu.VMEM(weight.shape, weight.dtype)] + shapes,
        in_specs=[ANYWHERE] + [IN_VMEM] * len(held) + [ANYWHERE] * len(after),
        out_specs=[IN_VMEM] * (1 + len(held)),
        scratch_shapes=[pltpu.SemaphoreType.DMA((parts,))],
        input_output_aliases=aliases,
        compiler_params=params(4),
        cost_estimate=cost(moved=weight.size * 2),
        name="load_weight",
    )(in_hbm(weight), *[in_vmem(a) for a in held], *after)
    return results[0], results[1:]


def pack(tokens, grad_out):
    own_rows, features = tokens.shape

    def kernel(tok_ref, grad_ref, out, stage, sems):
        copies = [
            pltpu.make_async_copy(ref, stage.at[i], sems.at[i])
            for i, ref in enumerate((tok_ref, grad_ref))
        ]
        for copy in copies:
            copy.start()
        for copy in copies:
            copy.wait()
        both = [stage[0].astype(F32), stage[1].astype(F32)]
        out[...] = jnp.concatenate(both, axis=0).astype(BF16)

    return pl.pallas_call(
        kernel,
        out_shape=pltpu.VMEM((2 * own_rows, features), BF16),
        in_specs=[ANYWHERE] * 2,
        out_specs=IN_VMEM,
        scratch_shapes=[
            pltpu.VMEM((2, own_rows, features), BF16),
            pltpu.SemaphoreType.DMA((2,)),
        ],
        compiler_params=params(4),
        name="pack",
    )(in_hbm(tokens), in_hbm(grad_out))


def join(own, near):
    both, features = own.shape
    own_rows = both // 2

    def kernel(own_ref, near_ref, out):
        pair = [own_ref[...].astype(F32), near_ref[...].astype(F32)]
        for g in range(2):
            half = slice(g * own_rows, (g + 1) * own_rows)
            out[g * both : (g + 1) * both, :] = jnp.concatenate(
                [p[half] for p in pair], axis=0
            ).astype(BF16)

    return pl.pallas_call(
        kernel,
        out_shape=pltpu.VMEM((2 * both, features), BF16),
        in_specs=[IN_VMEM] * 2,
        out_specs=IN_VMEM,
        compiler_params=params(4),
        name="join",
    )(own, near)


def unpack(blocks, held):
    n, w = len(blocks), len(held)
    rows, features = blocks[0].shape
    half = rows // 2

    def kernel(*refs):
        for b in range(n):
            for g in range(2):
                refs[n + w + g][b * half : (b + 1) * half, :] = refs[b][g * half : (g + 1) * half, :]

    shapes, aliases = through(held, n, 2)
    results = pl.pallas_call(
        kernel,
        out_shape=[pltpu.VMEM((n * half, features), BF16)] * 2 + shapes,
        in_specs=[IN_VMEM] * (n + w),
        out_specs=[IN_VMEM] * (2 + w),
        input_output_aliases=aliases,
        compiler_params=params(4),
        name="unpack",
    )(*blocks, *[in_vmem(a) for a in held])
    return results[0], results[1], results[2:]


def back_products(place, x, source, weights, groups):
    total = x.shape[0]
    share = total // groups
    hidden = source.shape[0]
    tile = tile_of(hidden, 1024)
    n, w = hidden // tile, len(weights)

    def kernel(place_ref, x_ref, src, *refs):
        outs, dst = refs[w : w + groups * n], refs[2 * w + groups * n - 1]
        acc, sems = refs[-2:]
        spans = [slice(b * tile, (b + 1) * tile) for b in range(n)]
        copies = [
            pltpu.make_async_copy(src.at[spans[b]], dst.at[spans[b]], sems.at[b]) for b in range(n)
        ]
        for copy in copies:
            copy.start()
        for b in range(n):
            copies[b].wait()
            acc[...] = contract_cols(x_ref[...], dst[spans[b], :])
            for j in range(groups):
                at = pl.multiple_of((place_ref[0] ^ j) * share, share)
                outs[j * n + b][...] = acc[pl.ds(at, share), :]

    shapes, aliases = through(weights, 3, groups * n)
    results = pl.pallas_call(
        kernel,
        out_shape=[pltpu.VMEM((share, tile), F32)] * (groups * n) + shapes,
        in_specs=[IN_SMEM, IN_VMEM, ANYWHERE] + [IN_VMEM] * w,
        out_specs=[IN_VMEM] * (groups * n + w),
        scratch_shapes=[pltpu.VMEM((total, tile), F32), pltpu.SemaphoreType.DMA((n,))],
        input_output_aliases=aliases,
        compiler_params=params(4),
        name="back_products",
    )(place, x, in_hbm(source), *[in_vmem(a) for a in weights])
    return [results[b : groups * n : n] for b in range(n)], results[groups * n :]


def first_products(place, x, weights, used, offset, width, groups, rest=None):
    total = x.shape[0]
    source = () if rest is None else (rest[0],)
    share = total // groups
    n, w = len(used), len(weights)

    def kernel(place_ref, x_ref, *refs):
        acc, sems = refs[-2:]
        copies = []
        if source:
            dst = refs[1 + w + groups + rest[1]]
            first = dst.shape[0] // rest[2]
            step = (dst.shape[0] - first) // 4
            for i in range(4):
                rows = pl.ds(first + i * step, step)
                copies.append(pltpu.make_async_copy(refs[0].at[rows], dst.at[rows], sems.at[i]))
                copies[-1].start()
        refs = refs[len(source) :]
        outs = refs[w : w + groups]
        for g in range(n):
            acc[...] = jnp.dot(
                x_ref[...],
                refs[used[g]][:, offset : offset + width],
                preferred_element_type=F32,
            )
            for j in range(groups):
                at = pl.multiple_of((place_ref[0] ^ j) * share, share)
                outs[j][:, g * width : (g + 1) * width] = acc[pl.ds(at, share), :]
        for copy in copies:
            copy.wait()

    shapes, aliases = through(weights, 2 + len(source), groups)
    results = pl.pallas_call(
        kernel,
        out_shape=[pltpu.VMEM((share, n * width), F32)] * groups + shapes,
        in_specs=[IN_SMEM, IN_VMEM] + [ANYWHERE] * len(source) + [IN_VMEM] * w,
        out_specs=[IN_VMEM] * (groups + w),
        scratch_shapes=[pltpu.VMEM((total, width), F32), pltpu.SemaphoreType.DMA((4,))],
        input_output_aliases=aliases,
        compiler_params=params(4),
        name="first_products",
    )(place, x, *[in_hbm(a) for a in source], *[in_vmem(a) for a in weights])
    return results[:groups], results[groups:]


def core_sum(pieces, weights):
    widths = [parts[0].shape[1] for parts in pieces]
    share, columns = pieces[0][0].shape[0], sum(widths)
    flat = [part for parts in pieces for part in parts]
    n, w, groups = len(flat), len(weights), len(pieces[0])

    def kernel(*refs):
        at = 0
        for p, width in enumerate(widths):
            total = refs[p * groups][...]
            for ref in refs[p * groups + 1 : (p + 1) * groups]:
                total = total + ref[...]
            refs[n + w][:, at : at + width] = total
            refs[n + w + 1][:, at : at + width] = total.astype(BF16)
            at += width

    shapes, aliases = through(weights, n, 2)
    results = pl.pallas_call(
        kernel,
        out_shape=[pltpu.VMEM((share, columns), F32), pltpu.VMEM((share, columns), BF16)] + shapes,
        in_specs=[IN_VMEM] * (n + w),
        out_specs=[IN_VMEM] * (2 + w),
        input_output_aliases=aliases,
        compiler_params=params(4),
        name="core_sum",
    )(*flat, *[in_vmem(a) for a in weights])
    return results[:2], results[2:]


def added(refs, cols):
    total = refs[0][:, cols]
    for ref in refs[1:]:
        total = total + ref[:, cols].astype(F32)
    return total


def hidden_units(terms, held):
    n, w = len(terms[0]), len(held)
    share, hidden = terms[0][0].shape
    step = tile_of(hidden, 512)

    def kernel(*refs):
        for at in range(0, hidden, step):
            gate_pre = added(refs[:n], slice(at, at + step))
            up_proj = added(refs[n : 2 * n], slice(at, at + step))
            sigmoid_gate = 1.0 / (1.0 + jnp.exp(-gate_pre))
            refs[2 * n + w][:, at : at + step] = (gate_pre * sigmoid_gate * up_proj).astype(BF16)

    shapes, aliases = through(held, 2 * n, 1)
    results = pl.pallas_call(
        kernel,
        out_shape=[pltpu.VMEM((share, hidden), BF16)] + shapes,
        in_specs=[IN_VMEM] * (2 * n + w),
        out_specs=[IN_VMEM] * (1 + w),
        input_output_aliases=aliases,
        compiler_params=params(4),
        name="hidden_units",
    )(*terms[0], *terms[1], *[in_vmem(a) for a in held])
    return results[0], results[1:]


def gate_grads(terms, back_terms, held):
    n, w = len(back_terms), len(held)
    share, hidden = back_terms[0].shape
    columns = 2 * hidden
    step = tile_of(hidden, 512)

    def kernel(*refs):
        out = refs[3 * n + w]
        for at in range(0, hidden, step):
            here, there = slice(at, at + step), slice(hidden + at, hidden + at + step)
            gate_pre, up_proj = added(refs[:n], here), added(refs[n : 2 * n], here)
            d_hidden = added(refs[2 * n : 3 * n], here)
            sigmoid_gate = 1.0 / (1.0 + jnp.exp(-gate_pre))
            out[:, here] = (
                d_hidden * up_proj * sigmoid_gate * (1.0 + gate_pre * (1.0 - sigmoid_gate))
            ).astype(BF16)
            out[:, there] = (d_hidden * gate_pre * sigmoid_gate).astype(BF16)

    shapes, aliases = through(held, 3 * n, 1)
    results = pl.pallas_call(
        kernel,
        out_shape=[pltpu.VMEM((share, columns), BF16)] + shapes,
        in_specs=[IN_VMEM] * (3 * n + w),
        out_specs=[IN_VMEM] * (1 + w),
        input_output_aliases=aliases,
        compiler_params=params(4),
        name="gate_grads",
    )(*terms[0], *terms[1], *back_terms, *[in_vmem(a) for a in held])
    return results[0], results[1:]


def lay(place_ref, share_refs, laid):
    share = share_refs[0].shape[0]
    for j, ref in enumerate(share_refs):
        at = pl.multiple_of((place_ref[0] ^ j) * share, share)
        laid[pl.ds(at, share), :] = ref[...]


def output_terms(place, shares, grad_all, down, held):
    groups, w = len(shares), len(held)
    total = shares[0].shape[0] * groups
    hidden, features = down.shape
    tile = tile_of(hidden, 512)
    n = hidden // tile
    early = (n + 1) // 2
    step = tile_of(features, 512)

    def kernel(place_ref, *refs):
        grad_ref = refs[groups]
        out, grad_down, block = refs[groups + 2 + w : groups + 5 + w]
        laid, sems = refs[-2:]
        lay(place_ref, refs[:groups], laid)
        copies = []
        for i in range(n):
            rows = slice(i * tile, (i + 1) * tile)
            room = rows
            if i < early:
                term = jnp.dot(laid[:, rows], block[rows, :], preferred_element_type=F32)
                out[...] = out[...] + term if i else term
            else:
                room = slice((i - early) * tile, (i - early + 1) * tile)
                copies[i - early].wait()
            for at in range(0, features, step):
                block[room, at : at + step] = contract_rows(
                    laid[:, rows], grad_ref[:, at : at + step]
                ).astype(BF16)
            copies.append(pltpu.make_async_copy(block.at[room], grad_down.at[rows], sems.at[i]))
            copies[-1].start()
        for copy in copies[n - early :]:
            copy.wait()

    shapes, aliases = through([down, *held], groups + 2, 2)
    results = pl.pallas_call(
        kernel,
        out_shape=[
            pltpu.VMEM((total, features), F32),
            jax.ShapeDtypeStruct((hidden, features), BF16),
        ]
        + shapes,
        in_specs=[IN_SMEM] + [IN_VMEM] * (groups + 2 + w),
        out_specs=[IN_VMEM, ANYWHERE] + [IN_VMEM] * (1 + w),
        scratch_shapes=[pltpu.VMEM((total, hidden), BF16), pltpu.SemaphoreType.DMA((n,))],
        input_output_aliases=aliases,
        compiler_params=params(4),
        name="output_terms",
    )(place, *shares, grad_all, in_vmem(down), *[in_vmem(a) for a in held])
    return results[0], results[1], early * tile, results[2:]


def more_output_terms(place, shares, out_terms, first, down, held):
    groups, w = len(shares), len(held)
    total = shares[0].shape[0] * groups
    hidden, features = down.shape
    rows = slice(first, hidden)

    def kernel(place_ref, *refs):
        before, down_ref = refs[groups : groups + 2]
        out, laid = refs[groups + 2 + w], refs[-1]
        lay(place_ref, [ref.at[:, rows] for ref in refs[:groups]], laid)
        out[...] = before[...] + jnp.dot(laid[...], down_ref[rows, :], preferred_element_type=F32)

    shapes, aliases = through(held, groups + 3, 1)
    results = pl.pallas_call(
        kernel,
        out_shape=[pltpu.VMEM((total, features), F32)] + shapes,
        in_specs=[IN_SMEM] + [IN_VMEM] * (groups + 2 + w),
        out_specs=[IN_VMEM] * (1 + w),
        scratch_shapes=[pltpu.VMEM((total, hidden - first), BF16)],
        input_output_aliases=aliases,
        compiler_params=params(4),
        name="more_output_terms",
    )(place, *shares, out_terms, in_vmem(down), *[in_vmem(a) for a in held])
    return results[0], results[1:]


def input_terms(place, shares, gate, up, out_terms, own_rows):
    groups = len(shares)
    total = shares[0].shape[0] * groups
    features, hidden = gate.shape
    parts = total // own_rows
    tile = tile_of(features, 1024)

    def kernel(place_ref, *refs):
        gate_ref, up_ref, out_ref, laid, keep, send = refs[groups:]
        lay(place_ref, refs[:groups], laid)
        d_gate, d_up = laid[:, :hidden].T, laid[:, hidden:].T
        for at in range(0, features, tile):
            cols = slice(at, at + tile)
            back = jnp.dot(gate_ref[cols, :], d_gate, preferred_element_type=F32)
            back = back + jnp.dot(up_ref[cols, :], d_up, preferred_element_type=F32)
            back = back.T
            for b in range(parts):
                rows = slice(b * own_rows, (b + 1) * own_rows)
                both = jnp.concatenate([out_ref[rows, cols], back[rows]], axis=0)
                if b % 2:
                    send[b // 2, :, cols] = both.astype(BF16)
                else:
                    keep[b // 2, :, cols] = both

    shape = (parts // 2, 2 * own_rows, features)
    return pl.pallas_call(
        kernel,
        out_shape=[
            pltpu.VMEM((total, 2 * hidden), BF16),
            pltpu.VMEM(shape, F32),
            pltpu.VMEM(shape, BF16),
        ],
        in_specs=[IN_SMEM] + [IN_VMEM] * (groups + 3),
        out_specs=[IN_VMEM] * 3,
        compiler_params=params(4),
        name="input_terms",
    )(place, *shares, in_vmem(gate), in_vmem(up), out_terms)


def row_sum(keep, near, after):
    n = keep.shape[0]

    def kernel(keep_ref, near_ref, *refs):
        refs = refs[len(after) :]
        refs[0][...] = keep_ref[0] + near_ref[0].astype(F32)
        for j in range(1, n):
            refs[j][...] = (keep_ref[j] + near_ref[j].astype(F32)).astype(BF16)

    shape = keep.shape[1:]
    results = pl.pallas_call(
        kernel,
        out_shape=[pltpu.VMEM(shape, F32)] + [pltpu.VMEM(shape, BF16)] * (n - 1),
        in_specs=[IN_VMEM] * 2 + [ANYWHERE] * len(after),
        out_specs=[IN_VMEM] * n,
        compiler_params=params(4),
        name="row_sum",
    )(keep, near, *[in_hbm(a) for a in after])
    return results[0], results[1:]


def last_sum(total, far, after):
    n = len(far)
    both, features = total.shape

    def kernel(total_ref, *refs):
        outs = refs[n + len(after) :]
        value = total_ref[...]
        for ref in refs[:n]:
            value = value + ref[...].astype(F32)
        outs[0][...] = value[: both // 2].astype(BF16)
        outs[1][...] = value[both // 2 :].astype(BF16)

    return pl.pallas_call(
        kernel,
        out_shape=[jax.ShapeDtypeStruct((both // 2, features), BF16)] * 2,
        in_specs=[IN_VMEM] * (1 + n) + [ANYWHERE] * len(after),
        out_specs=[IN_VMEM] * 2,
        compiler_params=params(4),
        name="last_sum",
    )(total, *far, *[in_hbm(a) for a in after])


def outer_here(left, right, first, columns, after):
    rows = left.shape[1]
    step = tile_of(columns, 256)

    def kernel(left_ref, right_ref, *refs):
        out = refs[len(after)]

        @pl.loop(0, columns // step)
        def _(i):
            at = pl.multiple_of(i * step, step)
            out[:, pl.ds(at, step)] = contract_rows(
                left_ref[...], right_ref[:, pl.ds(first + at, step)]
            ).astype(BF16)

    return pl.pallas_call(
        kernel,
        out_shape=pltpu.VMEM((rows, columns), BF16),
        in_specs=[IN_VMEM] * 2 + [ANYWHERE] * len(after),
        out_specs=IN_VMEM,
        compiler_params=params(8),
        cost_estimate=cost(moved=rows * columns * 2),
        name="outer_here",
    )(left, right, *after)


def outer(left, right, first, columns, after):
    rows = left.shape[1]
    step = tile_of(columns, 512)
    blocks, at = [], 0
    for size in (128, 128, 256):
        if at + size < rows:
            blocks.append((at, size))
            at += size
    while at < rows:
        size = min(512, rows - at)
        blocks.append((at, size))
        at += size

    def kernel(left_ref, right_ref, *refs):
        out, stage, sems = refs[len(after) :]
        copies = []
        for i, (at, size) in enumerate(blocks):
            block = slice(at, at + size)
            for s in range(0, columns, step):
                stage[block, s : s + step] = contract_rows(
                    left_ref[:, block], right_ref[:, first + s : first + s + step]
                ).astype(BF16)
            copies.append(pltpu.make_async_copy(stage.at[block], out.at[block], sems.at[i]))
            copies[-1].start()
        for copy in copies:
            copy.wait()

    return pl.pallas_call(
        kernel,
        out_shape=jax.ShapeDtypeStruct((rows, columns), BF16),
        in_specs=[IN_VMEM] * 2 + [ANYWHERE] * len(after),
        out_specs=ANYWHERE,
        scratch_shapes=[
            pltpu.VMEM((rows, columns), BF16),
            pltpu.SemaphoreType.DMA((len(blocks),)),
        ],
        compiler_params=params(20),
        cost_estimate=cost(moved=rows * columns * 2),
        name="outer",
    )(left, right, *after)


def per_device(tokens, grad_out, gate_weight, up_weight, down_weight):
    own_rows = tokens.shape[0]
    rows, cores, chips = (lax.axis_size(a) for a in ("row", "depth", "col"))
    hidden = gate_weight.shape[1]
    place = lax.axis_index("depth").astype(jnp.int32).reshape(1)

    own = pack(tokens, grad_out)
    pair = join(own, swap(own, "row", 1))
    blocks = [pair] + [swap(pair, "row", k) for k in range(2, rows, 2)]
    gate, _ = load(gate_weight, [], (pair,))
    up, (gate,) = load(up_weight, [gate], (), 2)
    down, (gate, up,) = make_room(down_weight, [gate, up])
    tok_all, grad_all, held = unpack(blocks, [gate, up, down])

    def over_cores(parts):
        return [parts[0]] + [swap(parts[j], "depth", j) for j in range(1, cores)]

    def over_chips(sums):
        total, rounded = sums
        return [total] + [swap(rounded, "col", k) for k in range(1, chips)]

    parted, terms = [], []
    for which in (0, 1):
        rest = None if which else (up_weight, 1, 2)
        parts, held = first_products(place, tok_all, held, [which], 0, hidden, cores, rest)
        parted.append(over_cores(parts))
    for parts in parted:
        sums, held = core_sum([parts], held)
        terms.append(over_chips(sums))
    back_parts, held = back_products(place, grad_all, down_weight, held, cores)
    back_parts = [over_cores(parts) for parts in back_parts]
    acts, held = hidden_units(terms, held)
    shares = over_cores([acts] * cores)
    sums, (*held, down) = core_sum(back_parts, held)
    back_terms = over_chips(sums)
    out_terms, grad_down, first, held = output_terms(place, shares, grad_all, down, held)
    acts, (down, *held) = gate_grads(terms, back_terms, held)
    hid_shares, shares = shares, over_cores([acts] * cores)
    out_terms, (gate, up) = more_output_terms(place, hid_shares, out_terms, first, down, held)
    d_all, keep, send = input_terms(place, shares, gate, up, out_terms, own_rows)

    near = swap(send, "row", 1)
    grad_gate = outer(tok_all, d_all, 0, hidden, (send,))
    total, rounded = row_sum(keep, near, (grad_gate,))
    far = [swap(rounded[j - 1], "row", 2 * j) for j in range(1, rows // 2)]
    grad_up = outer(tok_all, d_all, hidden, hidden, (total,))
    layer_out, grad_tokens = last_sum(total, far, (grad_up,))
    return layer_out, grad_tokens, grad_gate, grad_up, grad_down


def solution(mesh):
    acts = P("row", ("col", "depth"))
    wide = P(("col", "depth"), "row")
    return jax.shard_map(
        per_device,
        mesh=mesh,
        in_specs=(acts, acts, wide, wide, acts),
        out_specs=(acts, acts, wide, wide, acts),
        check_vma=False,
    )
```
